512 devices in a mesh: cell: 8 (over z), donor: 8 (over x, core), gene: 8 (over y).
Axes of the slice: x: 4, y: 8, z: 8, core: 2. Of those that a mesh axis runs over, the one named last changes fastest.
Arguments:
- counts: int32 [32768, 2048], P(('cell', 'donor'), 'gene'), may hold values from 0 to 35
- cell_donor: int32 [32768], P(('cell', 'donor')), may hold values from 0 to 511, as said below
- cell_type: int32 [32768], P(('cell', 'donor')), may hold values from -1 to 23, as said below
- covariates: float32 [512, 50], P(('cell', 'donor')), may hold values from -6 to 6
- dosage: int32 [8192, 512], P('gene'), may hold values from 0 to 2
- windows: int32 [2048, 1024], P(('gene', 'cell', 'donor')), may hold values from -1 to 8191, as said below
Outputs:
- association: float32 [24, 2048, 1024], P(None, ('gene', 'cell', 'donor'))
The draws below stay inside these ranges and needn't reach their ends.
Inputs may be any that keep to these rules, and one draw needn't show every extreme that they name: `cell_donor`: rows come in blocks of 512: a row of block b names a donor d with (d // 8) % 8 = b % 8. Every donor has at least one cell of every cell type. `cell_type`: in each block of 512 rows the live slots (type 0 or more) come first and the empty ones (-1) last; the number of live slots varies from block to block and some block is full. `windows`: row j lists consecutive SNP numbers in ascending order, then -1 to its end; all of them lie in [b * 1024, (b + 1) * 1024) with b = j // 256. A window holds 512 to 1024 SNPs, some window holds exactly 1024, and the last gene's window ends at the last SNP.
All inputs are finite; a program needn't handle non-finite values.
Results may differ from the reference program's by a relative error of at most 0.00045.
Values sent between devices are 32-bit elements; how exact they have to be, the bound alone decides.
No kernel may reach another device: no remote copies, remote signals or barrier semaphores. Data moves between devices by JAX's collectives and lax.ppermute only.
A program may use at most 64 MiB of HBM per device.

```python
import math
import jax
import jax.numpy as jnp
from jax import lax

GENES = 2048
CT = 24
NCOV = 50
WIN = 1024
SNP_DEV = 1024
DON_GRP = 64
CELL_DEV = 512
DON_OWN = 8
DONORS = 512
CELLS = 32768
SNPS = 8192
N_CELL = 8
N_DONOR = 8
N_GENE = 8


def cell_labels(key):
    base_key = jax.random.fold_in(key, 11)
    key_live, key_full, key_cover, key_first, key_second, key_kind = jax.random.split(base_key, 6)
    block_count = N_CELL * N_DONOR
    per_device = DON_OWN * CT
    slot_index = jnp.arange(CELL_DEV, dtype=jnp.int32)[None, :]
    block_index = jnp.arange(block_count, dtype=jnp.int32)[:, None]
    group_index = block_index % N_DONOR
    cell_slot = block_index // N_DONOR
    lowest = min(CELL_DEV, max(CELL_DEV // 2, per_device))
    live_count = jax.random.randint(key_live, (block_count, 1), lowest, CELL_DEV + 1)
    full_block = jax.random.randint(key_full, (), 0, block_count)
    live_count = jnp.where(block_index == full_block, CELL_DEV, live_count)
    shuffled = jax.vmap(lambda sub_key: jax.random.permutation(sub_key, per_device))(jax.random.split(key_cover, block_count))
    covered = jnp.pad(cell_slot * per_device + shuffled.astype(jnp.int32), ((0, 0), (0, CELL_DEV - per_device)))
    first_pick = jax.random.randint(key_first, (block_count, CELL_DEV), 0, DON_GRP)
    second_pick = jax.random.randint(key_second, (block_count, CELL_DEV), 0, DON_GRP)
    kind_pick = jax.random.randint(key_kind, (block_count, CELL_DEV), 0, CT)
    chosen = jnp.minimum(first_pick, second_pick) * CT + kind_pick
    owner_slot = jnp.where(slot_index < per_device, covered, chosen)
    local_donor = owner_slot // CT
    kind = owner_slot % CT
    donor_id = (local_donor // DON_OWN * N_DONOR + group_index) * DON_OWN + local_donor % DON_OWN
    kind = jnp.where(slot_index < live_count, kind, -1)
    return (donor_id.reshape(-1).astype(jnp.int32), kind.reshape(-1).astype(jnp.int32))


def draw_cell_donor(key, part):
    return cell_labels(key)[0]


def draw_cell_type(key, part):
    return cell_labels(key)[1]


def draw_counts(key, part):
    base_key = jax.random.fold_in(key, 23)
    key_rate, key_value = jax.random.split(base_key, 2)
    gene_index = jnp.arange(GENES, dtype=jnp.int32)
    rate_base = jax.random.randint(key_rate, (GENES,), 4, 13)
    top_value = rate_base * (GENES + 2 * gene_index) // GENES
    return jax.random.randint(key_value, (CELLS, GENES), 0, top_value[None, :] + 1).astype(jnp.int32)


def draw_windows(key, part):
    base_key = jax.random.fold_in(key, 37)
    key_length, key_long, key_start = jax.random.split(base_key, 3)
    gene_index = jnp.arange(GENES, dtype=jnp.int32)
    lengths = jax.random.randint(key_length, (GENES,), WIN // 2, WIN + 1)
    longest = jax.random.randint(key_long, (), 0, GENES)
    lengths = jnp.where(gene_index == longest, WIN, lengths)
    starts = jax.random.randint(key_start, (GENES,), 0, SNP_DEV - lengths + 1)
    starts = jnp.where(gene_index == GENES - 1, SNP_DEV - lengths, starts)
    gene_group = gene_index // (GENES // N_GENE)
    position = jnp.arange(WIN, dtype=jnp.int32)[None, :]
    snp_number = gene_group[:, None] * SNP_DEV + starts[:, None] + position
    return jnp.where(position < lengths[:, None], snp_number, -1).astype(jnp.int32)


def set_ends(values, stream_key, smallest, high):
    spot = [jax.random.randint(jax.random.fold_in(stream_key, axis), (), 0, length) for axis, length in enumerate(values.shape)]
    widest = values.shape.index(max(values.shape))
    neighbour = spot[:widest] + [(spot[widest] + 1) % values.shape[widest]] + spot[widest + 1:]
    return values.at[tuple(spot)].set(smallest).at[tuple(neighbour)].set(high)


def block_scale(rng, dims, cuts, least, high):
    def one(dim, parts):
        draws = jax.random.uniform(jax.random.fold_in(jax.random.fold_in(rng, 6), dim), (parts,), jnp.float32, least / len(cuts), high / len(cuts))
        return jnp.repeat(jnp.exp(draws), dims[dim] // parts).reshape((-1,) + (1,) * (len(dims) - dim - 1))

    loudness = one(*cuts[0])
    for cut in cuts[1:]:
        loudness = loudness * one(*cut)
    return loudness


def normal_values(rng, dims, spread, bound, cuts=(), kind=jnp.bfloat16):
    loudness = block_scale(rng, dims, cuts, -0.22, 0.18) if cuts else 1.0
    drawn = jax.random.normal(rng, dims, jnp.float32) * spread * loudness
    return jnp.minimum(jnp.maximum(drawn, -bound), bound).astype(kind)


def setup_inputs(seed: int = 0) -> dict:
    key_list = jax.random.split(jax.random.key(seed), 7)
    return {
        "counts": draw_counts(jax.random.fold_in(key_list[6], 71), 0),
        "cell_donor": draw_cell_donor(jax.random.fold_in(key_list[6], 71), 0),
        "cell_type": draw_cell_type(jax.random.fold_in(key_list[6], 71), 0),
        "covariates": normal_values(key_list[3], (DONORS, NCOV), 1.0, 6.0, ((0, 64),), jnp.float32),
        "dosage": set_ends(jax.random.randint(key_list[4], (SNPS, DONORS), 0, 3), jax.random.fold_in(key_list[4], 1), 0, 2).astype(jnp.int32),
        "windows": draw_windows(jax.random.fold_in(key_list[6], 71), 0),
    }


def log_cpm(pseudobulk, library):
    return jnp.log2((pseudobulk + 0.5) / (library + 1.0) * 1000000.0)

def with_intercept(covariates):
    intercept = jnp.ones((covariates.shape[0], 1), jnp.float32)
    return jnp.concatenate([intercept, covariates.astype(jnp.float32)], axis=1)

def factor_lower(gram_sum):
    order = gram_sum.shape[0]
    factor = jnp.zeros_like(gram_sum)
    for column in range(order):
        known = factor[column, :column]
        pivot = jnp.sqrt(gram_sum[column, column] - jnp.sum(known * known))
        factor = factor.at[column, column].set(pivot)
        if column + 1 < order:
            below = gram_sum[column + 1:, column] - jnp.dot(factor[column + 1:, :column], known, precision=lax.Precision.HIGHEST)
            factor = factor.at[column + 1:, column].set(below / pivot)
    return factor

def solve_written(factor, right_rows):
    order = factor.shape[0]
    forward = []
    for row in range(order):
        value = right_rows[row]
        if row > 0:
            value = value - jnp.dot(factor[row, :row], jnp.stack(forward), precision=lax.Precision.HIGHEST)
        forward.append(value / factor[row, row])
    backward = [None] * order
    for row in range(order - 1, -1, -1):
        value = forward[row]
        if row < order - 1:
            later = jnp.stack(backward[row + 1:])
            value = value - jnp.dot(factor[row + 1:, row], later, precision=lax.Precision.HIGHEST)
        backward[row] = value / factor[row, row]
    return jnp.stack(backward)

def solve_normal(gram_sum, cross_sum):
    order = gram_sum.shape[0]
    factor = factor_lower(gram_sum)
    inverse = solve_written(factor, jnp.eye(order, dtype=jnp.float32))
    return jnp.einsum('kj,cjg->ckg', inverse, cross_sum, precision=lax.Precision.HIGHEST)

def residualize_local(expression, covariates):
    design = with_intercept(covariates)
    gram_sum = jnp.dot(design.T, design, precision=lax.Precision.HIGHEST)
    cross_sum = jnp.einsum('dk,dcg->ckg', design, expression, precision=lax.Precision.HIGHEST)
    coefficients = solve_normal(gram_sum, cross_sum)
    return expression - jnp.einsum('dk,ckg->dcg', design, coefficients, precision=lax.Precision.HIGHEST)

def association_block(residual, dosage, windows, first_snp):
    live_window = windows >= 0
    row_ids = jnp.where(live_window, windows - first_snp, 0).astype(jnp.int32)
    picked = jnp.take(dosage, row_ids, axis=0).astype(jnp.float32)
    products = jnp.einsum('gwd,dcg->cgw', picked, residual, precision=lax.Precision.HIGHEST)
    scaling = 1.0 / math.sqrt(dosage.shape[1])
    return jnp.where(live_window[None], products, 0.0) * scaling

def reference(counts, cell_donor, cell_type, covariates, dosage, windows):
    owner_total = DONORS * CT
    owner_slot = jnp.where(cell_type >= 0, cell_donor * CT + cell_type, owner_total).astype(jnp.int32)
    count_blocks = counts.reshape(-1, CELL_DEV, GENES)
    owner_blocks = owner_slot.reshape(-1, CELL_DEV)

    def add_block(running, block_pair):
        block_counts, block_owner = block_pair
        summed = jax.ops.segment_sum(block_counts.astype(jnp.float32), block_owner, num_segments=owner_total + 1)
        return (running + summed, None)
    start_total = jnp.zeros((owner_total + 1, GENES), jnp.float32)
    running, _ = lax.scan(add_block, start_total, (count_blocks, owner_blocks))
    pseudobulk = running[:owner_total].reshape(DONORS, CT, GENES)
    library = lax.optimization_barrier(jnp.sum(pseudobulk, axis=2, keepdims=True))
    expression = log_cpm(pseudobulk, library)
    residual = residualize_local(expression, covariates)
    gene_block = 64
    residual_blocks = jnp.transpose(residual.reshape(DONORS, CT, GENES // gene_block, gene_block), (2, 0, 1, 3))
    window_blocks = windows.reshape(GENES // gene_block, gene_block, WIN)
    result = lax.map(lambda pieces: association_block(pieces[0], dosage, pieces[1], 0), (residual_blocks, window_blocks))
    return jnp.transpose(result, (1, 0, 2, 3)).reshape(CT, GENES, WIN)
```

```python
import math

import jax
import jax.numpy as jnp
from jax import lax
from jax.experimental import pallas as pl
from jax.experimental.pallas import tpu as pltpu
from jax.sharding import PartitionSpec as P

F32 = jnp.float32
BF16 = jnp.bfloat16
I32 = jnp.int32
HIGHEST = lax.Precision.HIGHEST

CT = 24
HALF = CT // 2
NCOV = 50
ORDER = NCOV + 1
N = 8
CELLS = 512
LANES = 128
CHUNKS = CELLS // LANES
GENES = 256
GENE_PART = GENES // N
OWN = GENE_PART // N
DON_GRP = 64
DONORS = N * DON_GRP
SNPS = 1024
WIN = 1024
LABEL_ROW = CHUNKS * GENE_PART
PART_ROWS = LABEL_ROW + 2 * CHUNKS
SUM_ROWS = HALF * GENE_PART
LIB_ROWS = 16

NT = (((1,), (1,)), ((), ()))


def split3(value):
    high = value.astype(BF16)
    rest = value - high.astype(F32)
    middle = rest.astype(BF16)
    low = (rest - middle.astype(F32)).astype(BF16)
    return high, middle, low


def pack_kernel(counts_ref, donor_ref, type_ref, part_ref, total_ref):
    donor = donor_ref[...].astype(F32)
    kind = type_ref[...].astype(F32)
    labels = jnp.concatenate([donor, kind], axis=0)
    totals = []
    for chunk in range(CHUNKS):
        rows = counts_ref[chunk * LANES : (chunk + 1) * LANES, :].astype(F32)
        turned = rows.T
        totals.append(jnp.sum(turned, axis=0, keepdims=True))
        for peer in range(N):
            part_ref[peer, chunk * GENE_PART : (chunk + 1) * GENE_PART, :] = turned[
                peer * GENE_PART : (peer + 1) * GENE_PART
            ]
    for peer in range(N):
        part_ref[peer, LABEL_ROW:PART_ROWS, :] = labels
    total = jnp.concatenate(totals, axis=0)
    total_ref[...] = jnp.broadcast_to(total[None], total_ref.shape)


def to_row(block):
    return jnp.concatenate([block[row : row + 1] for row in range(CHUNKS)], axis=1)


def expression_kernel(part_ref, total_ref, out_ref, sum_ref):
    sum_ref[...] = jnp.zeros_like(sum_ref)

    def one_block(block, carry):
        labels = part_ref[block, LABEL_ROW:PART_ROWS, :]
        donor = to_row(labels[:CHUNKS]).astype(I32)
        kind = to_row(labels[CHUNKS:]).astype(I32)
        local = ((donor >> 6) << 3) + (donor & 7)
        upper = kind >= HALF
        column = jnp.where(kind >= 0, jnp.where(upper, local + DON_GRP, local), -1)
        step = jnp.where(upper, kind - HALF, kind)
        place = lax.broadcasted_iota(I32, (LANES, CELLS), 0)
        onehot = jnp.where(place == column, 1.0, 0.0).astype(BF16)
        counts = jnp.concatenate(
            [
                part_ref[block, chunk * GENE_PART : (chunk + 1) * GENE_PART, :]
                for chunk in range(CHUNKS)
            ],
            axis=1,
        )
        step_full = jnp.broadcast_to(step, (GENE_PART, CELLS))
        pieces = [
            jnp.where(step_full == number, counts, 0.0).astype(BF16) for number in range(HALF)
        ]
        total = total_ref[block * N]
        for gene in range(1, N):
            total = total + total_ref[block * N + gene]
        total = to_row(total)
        number = lax.broadcasted_iota(I32, (LIB_ROWS, CELLS), 0)
        wanted = number == step
        for piece in split3(total):
            pieces.append(jnp.where(wanted, piece.astype(F32), 0.0).astype(BF16))
        left = jnp.concatenate(pieces, axis=0)
        sum_ref[...] += lax.dot_general(left, onehot, NT, preferred_element_type=F32)
        return carry

    lax.fori_loop(0, N, one_block, 0)
    library = (
        sum_ref[SUM_ROWS : SUM_ROWS + LIB_ROWS]
        + sum_ref[SUM_ROWS + LIB_ROWS : SUM_ROWS + 2 * LIB_ROWS]
        + sum_ref[SUM_ROWS + 2 * LIB_ROWS : SUM_ROWS + 3 * LIB_ROWS]
    )
    for step in range(HALF):
        summed = sum_ref[step * GENE_PART : (step + 1) * GENE_PART, :]
        expression = jnp.log2((summed + 0.5) / (library[step : step + 1] + 1.0) * 1000000.0)
        for peer in range(N):
            out_ref[peer, step * OWN : (step + 1) * OWN, :] = expression[
                peer * OWN : (peer + 1) * OWN
            ]


def projection_kernel(cov_ref, dosage_ref, high_ref, middle_ref, low_ref, dosage_out_ref):
    dosage_out_ref[...] = dosage_ref[...].astype(F32).astype(BF16)
    lane = lax.broadcasted_iota(I32, (DONORS, LANES), 1)
    natural = jnp.where(lane == NCOV, 1.0, cov_ref[...].reshape(DONORS, LANES))
    grouped = jnp.concatenate(
        [cov_ref[cell * N + donor] for donor in range(N) for cell in range(N)], axis=0
    )
    grouped = jnp.where(lane == NCOV, 1.0, grouped)
    turned = natural.T
    gram = lax.dot_general(turned, turned, NT, precision=HIGHEST, preferred_element_type=F32)
    rows = 56
    row_id = lax.broadcasted_iota(I32, (rows, LANES), 0)
    lane_id = lax.broadcasted_iota(I32, (rows, LANES), 1)
    work = jnp.where(lane_id < 64, gram[:rows], jnp.where(lane_id - 64 == row_id, 1.0, 0.0))
    row_col = lax.broadcasted_iota(I32, (rows, 1), 0)
    for column in range(ORDER):
        pivot_row = work[column : column + 1, :]
        scaled = pivot_row / pivot_row[:, column : column + 1]
        below = jnp.where(row_col > column, work[:, column : column + 1], 0.0)
        work = work - below * scaled
    pivots = jnp.sum(jnp.where(lane_id == row_id, work, 0.0), axis=1, keepdims=True)
    scale = 1.0 / jnp.sqrt(jnp.where(row_col < ORDER, pivots, 1.0))
    inverse = pltpu.roll(work, 64, 1)
    inverse = jnp.where((lane_id < ORDER) & (row_id < ORDER), inverse * scale, 0.0)
    left = lax.dot_general(grouped, inverse, NT, precision=HIGHEST, preferred_element_type=F32)
    right = lax.dot_general(
        inverse, turned, (((1,), (0,)), ((), ())), precision=HIGHEST, preferred_element_type=F32
    )
    span = 128
    for start in range(0, DONORS, span):
        row = lax.broadcasted_iota(I32, (span, DONORS), 0) + start
        column = lax.broadcasted_iota(I32, (span, DONORS), 1)
        same = (((row >> 3) & 7) << 6) + ((row >> 6) << 3) + (row & 7) == column
        fitted = lax.dot_general(
            left[start : start + span],
            right,
            (((1,), (0,)), ((), ())),
            precision=HIGHEST,
            preferred_element_type=F32,
        )
        kept = jnp.where(same, 1.0, 0.0) - fitted
        high, middle, low = split3(kept)
        high_ref[start : start + span, :] = high
        middle_ref[start : start + span, :] = middle
        low_ref[start : start + span, :] = low


def association_kernel(
    expr_ref, high_ref, middle_ref, low_ref, dosage_ref, windows_ref, first_ref, out_ref
):
    rows = HALF * OWN
    lane = lax.broadcasted_iota(I32, (rows, LANES), 1)
    lower, upper = [], []
    for pair in range(N // 2):
        one, two = expr_ref[2 * pair], expr_ref[2 * pair + 1]
        lower.append(jnp.where(lane < 64, one, pltpu.roll(two, 64, 1)))
        upper.append(jnp.where(lane < 64, pltpu.roll(one, 64, 1), two))
    expression = jnp.concatenate(
        [jnp.concatenate(lower, axis=1), jnp.concatenate(upper, axis=1)], axis=0
    )
    both = 2 * rows
    parts = jnp.concatenate(split3(expression), axis=0)
    plain = (((1,), (0,)), ((), ()))
    first = lax.dot_general(parts, high_ref[...], plain, preferred_element_type=F32)
    second = lax.dot_general(parts[: 2 * both], middle_ref[...], plain, preferred_element_type=F32)
    third = lax.dot_general(parts[:both], low_ref[...], plain, preferred_element_type=F32)
    residual = (
        (third + second[both:] + first[2 * both :]) + (second[:both] + first[both : 2 * both])
    ) + first[:both]
    upper_part = residual.astype(BF16)
    lower_part = (residual - upper_part.astype(F32)).astype(BF16)
    products = lax.dot_general(
        jnp.concatenate([upper_part, lower_part], axis=0),
        dosage_ref[...],
        NT,
        preferred_element_type=F32,
    )
    products = (products[:both] + products[both:]) * (1.0 / math.sqrt(DONORS))
    gene_of_row = lax.broadcasted_iota(I32, (both, WIN), 0) & (OWN - 1)
    windows = windows_ref[...]
    result = jnp.zeros_like(products)
    for gene in range(OWN):
        start = first_ref[gene] & (SNPS - 1)
        turned = pltpu.roll(products, (SNPS - start) & (SNPS - 1), 1)
        live = windows[gene : gene + 1] >= 0
        result = jnp.where((gene_of_row == gene) & live, turned, result)
    for kind in range(CT):
        out_ref[kind] = result[kind * OWN : (kind + 1) * OWN]


VMEM = pl.BlockSpec(memory_space=pltpu.VMEM)
SMEM = pl.BlockSpec(memory_space=pltpu.SMEM)
PARAMS = pltpu.CompilerParams(vmem_limit_bytes=48 * 1024 * 1024)


def call(kernel, name, outs, n_in, scratch=(), smem_last=False):
    specs = [VMEM] * n_in
    if smem_last:
        specs[-1] = SMEM
    return pl.pallas_call(
        kernel,
        name=name,
        out_shape=outs,
        in_specs=specs,
        out_specs=jax.tree.map(lambda _: VMEM, outs),
        scratch_shapes=scratch,
        compiler_params=PARAMS,
    )


def shape(*dims, dtype=F32):
    return jax.ShapeDtypeStruct(dims, dtype)


pack = call(pack_kernel, "pack", [shape(N, PART_ROWS, LANES), shape(N * N, CHUNKS, LANES)], 3)
express = call(
    expression_kernel,
    "express",
    shape(N, HALF * OWN, LANES),
    2,
    [pltpu.VMEM((SUM_ROWS + 3 * LIB_ROWS, LANES), F32)],
)
project = call(
    projection_kernel,
    "project",
    [shape(DONORS, DONORS, dtype=BF16)] * 3 + [shape(SNPS, DONORS, dtype=BF16)],
    2,
)
associate = call(
    association_kernel, "associate", shape(CT, OWN, WIN), 7, smem_last=True
)


def per_device(counts, cell_donor, cell_type, covariates, dosage, windows):
    parts, totals = pack(
        counts, cell_donor.reshape(CHUNKS, LANES), cell_type.reshape(CHUNKS, LANES)
    )
    parts = lax.all_to_all(parts, "cell", 0, 0, tiled=True)
    totals = lax.all_to_all(totals, ("cell", "gene"), 0, 0, tiled=True)
    padded = jnp.pad(covariates, ((0, 0), (0, LANES - NCOV)))
    every = lax.all_to_all(
        jnp.broadcast_to(padded[None], (N * N,) + padded.shape),
        ("cell", "donor"),
        0,
        0,
        tiled=True,
    )
    high, middle, low, dosage_half = project(every, dosage)
    expression = express(parts, totals)
    expression = lax.all_to_all(expression, "donor", 0, 0, tiled=True)
    return associate(expression, high, middle, low, dosage_half, windows, windows[:, 0])


def solution(mesh):
    in_specs = (
        P(("cell", "donor"), "gene"),
        P(("cell", "donor")),
        P(("cell", "donor")),
        P(("cell", "donor"), None),
        P("gene", None),
        P(("gene", "cell", "donor"), None),
    )
    out_specs = P(None, ("gene", "cell", "donor"), None)
    return jax.shard_map(
        per_device, mesh=mesh, in_specs=in_specs, out_specs=out_specs, check_vma=False
    )
```

```python
import math

import jax
import jax.numpy as jnp
from jax import lax
from jax.experimental import pallas as pl
from jax.experimental.pallas import tpu as pltpu
from jax.sharding import PartitionSpec as P

F32 = jnp.float32
BF16 = jnp.bfloat16
I32 = jnp.int32
HIGHEST = lax.Precision.HIGHEST

CT = 24
SUB = 8
PARTS = CT // SUB
NCOV = 50
ORDER = NCOV + 1
N = 8
PEERS = N * N
CELLS = 512
LANES = 128
CHUNKS = CELLS // LANES
GENES = 256
OWN = GENES // PEERS
DON_GRP = 64
DONORS = N * DON_GRP
SNPS = 1024
WIN = 1024
ROWS = 32
DONOR_ROW = CHUNKS * OWN
TYPE_ROW = DONOR_ROW + CHUNKS
TOTAL_ROW = TYPE_ROW + CHUNKS
COV_ROW = TOTAL_ROW + CHUNKS
KINDS = OWN + 2

NT = (((1,), (1,)), ((), ()))


def split3(value):
    high = value.astype(BF16)
    rest = value - high.astype(F32)
    middle = rest.astype(BF16)
    low = (rest - middle.astype(F32)).astype(BF16)
    return high, middle, low


def pack_kernel(
    counts_hbm, donor_hbm, type_hbm, cov_hbm, part_ref,
    counts_ref, donor_ref, type_ref, cov_ref, wide_ref, sems,
):
    copies = [
        pltpu.make_async_copy(
            counts_hbm.at[pl.ds(chunk * LANES, LANES)],
            counts_ref.at[pl.ds(chunk * LANES, LANES)],
            sems.at[chunk],
        )
        for chunk in range(CHUNKS)
    ]
    copies.append(pltpu.make_async_copy(donor_hbm, donor_ref, sems.at[CHUNKS]))
    copies.append(pltpu.make_async_copy(type_hbm, type_ref, sems.at[CHUNKS + 1]))
    copies.append(pltpu.make_async_copy(cov_hbm, cov_ref, sems.at[CHUNKS + 2]))
    for copy in copies:
        copy.start()
    totals = []
    for chunk in range(CHUNKS):
        copies[chunk].wait()
        turned = counts_ref[chunk * LANES : (chunk + 1) * LANES, :].astype(F32).T
        totals.append(jnp.sum(turned, axis=0, keepdims=True))
        for peer in range(PEERS):
            part_ref[peer, chunk * OWN : (chunk + 1) * OWN, :] = turned[
                peer * OWN : (peer + 1) * OWN
            ]
    for copy in copies[CHUNKS:]:
        copy.wait()
    wide_ref[...] = jnp.zeros_like(wide_ref)
    wide_ref[:, :NCOV] = cov_ref[...]
    wide = wide_ref[...]
    paired = wide[: N // 2] + pltpu.roll(wide, DON_GRP, 1)[N // 2 :]
    shared = jnp.concatenate(
        [donor_ref[...].astype(F32), type_ref[...].astype(F32), *totals, paired], axis=0
    )
    for peer in range(PEERS):
        part_ref[peer, DONOR_ROW:ROWS, :] = shared


def to_row(block):
    return jnp.concatenate([block[row : row + 1] for row in range(CHUNKS)], axis=1)


def sum_kernel(part_ref, sum_ref, library_ref):
    lane = lax.broadcasted_iota(I32, (KINDS * SUB, LANES), 1)

    def one_block(block):
        block_rows = part_ref[block]
        donor = to_row(block_rows[DONOR_ROW:TYPE_ROW]).astype(I32)
        kind = to_row(block_rows[TYPE_ROW:TOTAL_ROW]).astype(I32)
        local = ((donor >> 6) << 3) + (donor & 7)
        column = jnp.where(kind >= 0, ((kind >> 3) << 6) + local, -1)
        place = lax.broadcasted_iota(I32, (PARTS * DON_GRP, CELLS), 0)
        onehot = jnp.where(place == column, 1.0, 0.0).astype(BF16)
        wanted = lax.broadcasted_iota(I32, (SUB, CELLS), 0) == (kind & 7)
        total = to_row(block_rows[TOTAL_ROW:COV_ROW])
        high = total.astype(BF16).astype(F32)
        values = [
            jnp.concatenate(
                [
                    block_rows[chunk * OWN + gene : chunk * OWN + gene + 1]
                    for chunk in range(CHUNKS)
                ],
                axis=1,
            )
            for gene in range(OWN)
        ]
        values += [high, total - high]
        left = jnp.concatenate([jnp.where(wanted, value, 0.0) for value in values], axis=0)
        return lax.dot_general(left.astype(BF16), onehot, NT, preferred_element_type=F32)

    def one_pair(pair, carry):
        even, odd = one_block(2 * pair), one_block(2 * pair + 1)
        for cell in range(1, N):
            even = even + one_block(cell * N + 2 * pair)
            odd = odd + one_block(cell * N + 2 * pair + 1)
        even_low, odd_low = even[:, :LANES], odd[:, :LANES]
        merged = [
            jnp.where(lane < DON_GRP, even_low, pltpu.roll(odd_low, DON_GRP, 1)),
            jnp.where(lane < DON_GRP, pltpu.roll(even_low, DON_GRP, 1), odd_low),
            jnp.concatenate([even[:, LANES:], odd[:, LANES:]], axis=1),
        ]
        span = pl.ds(pl.multiple_of(pair * LANES, LANES), LANES)
        for part, value in enumerate(merged):
            for gene in range(OWN):
                start = gene * CT + part * SUB
                sum_ref[start : start + SUB, span] = value[gene * SUB : (gene + 1) * SUB]
            library = value[OWN * SUB : (OWN + 1) * SUB] + value[(OWN + 1) * SUB :]
            for peer in range(N):
                library_ref[peer, part * SUB : (part + 1) * SUB, span] = library
        return carry

    lax.fori_loop(0, N // 2, one_pair, 0)


def projection_kernel(part_ref, dosage_ref, high_ref, middle_ref, low_ref, dosage_out_ref):
    dosage_out_ref[...] = dosage_ref[...].astype(F32).astype(BF16)
    lane = lax.broadcasted_iota(I32, (SUB, LANES), 1)
    first_half = lax.broadcasted_iota(I32, (SUB, LANES), 0) < N // 2
    tiles = []
    for block in range(PEERS):
        tile = part_ref[block, TOTAL_ROW:ROWS, :]
        rows = jnp.where(first_half, pltpu.roll(tile, N // 2, 0), pltpu.roll(tile, DON_GRP, 1))
        tiles.append(jnp.where(lane < NCOV, rows, jnp.where(lane == NCOV, 1.0, 0.0)))
    natural = jnp.concatenate(tiles, axis=0)
    grouped = jnp.concatenate(
        [tiles[cell * N + donor] for donor in range(N) for cell in range(N)], axis=0
    )
    turned = natural.T
    gram = lax.dot_general(turned, turned, NT, precision=HIGHEST, preferred_element_type=F32)
    rows = 56
    row_id = lax.broadcasted_iota(I32, (rows, LANES), 0)
    lane_id = lax.broadcasted_iota(I32, (rows, LANES), 1)
    work = jnp.where(lane_id < 64, gram[:rows], jnp.where(lane_id - 64 == row_id, 1.0, 0.0))
    row_col = lax.broadcasted_iota(I32, (rows, 1), 0)
    for column in range(ORDER):
        pivot_row = work[column : column + 1, :]
        scaled = pivot_row / pivot_row[:, column : column + 1]
        below = jnp.where(row_col > column, work[:, column : column + 1], 0.0)
        work = work - below * scaled
    pivots = jnp.sum(jnp.where(lane_id == row_id, work, 0.0), axis=1, keepdims=True)
    scale = 1.0 / jnp.sqrt(jnp.where(row_col < ORDER, pivots, 1.0))
    inverse = pltpu.roll(work, 64, 1)
    inverse = jnp.where((lane_id < ORDER) & (row_id < ORDER), inverse * scale, 0.0)
    left = lax.dot_general(grouped, inverse, NT, precision=HIGHEST, preferred_element_type=F32)
    right = lax.dot_general(
        inverse, turned, (((1,), (0,)), ((), ())), precision=HIGHEST, preferred_element_type=F32
    )
    span = 128
    for start in range(0, DONORS, span):
        row = lax.broadcasted_iota(I32, (span, DONORS), 0) + start
        column = lax.broadcasted_iota(I32, (span, DONORS), 1)
        same = (((row >> 3) & 7) << 6) + ((row >> 6) << 3) + (row & 7) == column
        fitted = lax.dot_general(
            left[start : start + span],
            right,
            (((1,), (0,)), ((), ())),
            precision=HIGHEST,
            preferred_element_type=F32,
        )
        kept = jnp.where(same, 1.0, 0.0) - fitted
        high, middle, low = split3(kept)
        high_ref[start : start + span, :] = high
        middle_ref[start : start + span, :] = middle
        low_ref[start : start + span, :] = low


def association_kernel(
    sum_hbm, library_ref, high_hbm, middle_hbm, low_hbm, dosage_hbm, windows_ref, out_ref,
    sum_ref, high_ref, middle_ref, low_ref, dosage_ref, sems,
):
    pairs = (
        (sum_hbm, sum_ref),
        (high_hbm, high_ref),
        (middle_hbm, middle_ref),
        (low_hbm, low_ref),
        (dosage_hbm, dosage_ref),
    )
    copies = [
        pltpu.make_async_copy(source, target, sems.at[index])
        for index, (source, target) in enumerate(pairs)
    ]
    for copy in copies:
        copy.start()
    library = library_ref[0]
    for peer in range(1, N):
        library = library + library_ref[peer]
    library = library + 1.0
    copies[0].wait()
    expression = jnp.concatenate(
        [
            jnp.log2((sum_ref[gene * CT : (gene + 1) * CT] + 0.5) / library * 1000000.0)
            for gene in range(OWN)
        ],
        axis=0,
    )
    both = OWN * CT
    parts = jnp.concatenate(split3(expression), axis=0)
    plain = (((1,), (0,)), ((), ()))
    for copy in copies[1:]:
        copy.wait()
    first = lax.dot_general(parts, high_ref[...], plain, preferred_element_type=F32)
    second = lax.dot_general(parts[: 2 * both], middle_ref[...], plain, preferred_element_type=F32)
    third = lax.dot_general(parts[:both], low_ref[...], plain, preferred_element_type=F32)
    residual = (
        (third + second[both:] + first[2 * both :]) + (second[:both] + first[both : 2 * both])
    ) + first[:both]
    upper_part = residual.astype(BF16)
    lower_part = (residual - upper_part.astype(F32)).astype(BF16)
    products = lax.dot_general(
        jnp.concatenate([upper_part, lower_part], axis=0),
        dosage_ref[...],
        NT,
        preferred_element_type=F32,
    )
    products = (products[:both] + products[both:]) * (1.0 / math.sqrt(DONORS))
    windows = windows_ref[...]
    lane = lax.broadcasted_iota(I32, (1, LANES), 1)
    for gene in range(OWN):
        first = jnp.where(lane == 0, windows[gene : gene + 1, :LANES], 0).astype(F32)
        start = jnp.sum(first).astype(I32) & (SNPS - 1)
        turned = pltpu.roll(
            products[gene * CT : (gene + 1) * CT], (SNPS - start) & (SNPS - 1), 1
        )
        live = windows[gene : gene + 1] >= 0
        out_ref[:, gene, :] = jnp.where(live, turned, 0.0)


MIB = 1024 * 1024
HBM = pl.BlockSpec(memory_space=pltpu.HBM)


def whole(dims):
    return pl.BlockSpec(dims, lambda step: (0,) * len(dims))


def call(kernel, name, outs, ins, limit, scratch=()):
    return pl.pallas_call(
        kernel,
        name=name,
        grid=(1,),
        out_shape=outs,
        in_specs=ins,
        out_specs=[whole(out.shape) for out in outs],
        scratch_shapes=scratch,
        compiler_params=pltpu.CompilerParams(vmem_limit_bytes=limit * MIB),
    )


PART_SHAPE = (PEERS, ROWS, LANES)
LIBRARY_SHAPE = (N, CT, DONORS)
SUM_SHAPE = (OWN * CT, DONORS)
SQUARE = (DONORS, DONORS)
DOSAGE_SHAPE = (SNPS, DONORS)

pack = call(
    pack_kernel,
    "pack",
    [jax.ShapeDtypeStruct(PART_SHAPE, F32)],
    [HBM] * 4,
    16,
    [
        pltpu.VMEM((CELLS, GENES), I32),
        pltpu.VMEM((CHUNKS, LANES), I32),
        pltpu.VMEM((CHUNKS, LANES), I32),
        pltpu.VMEM((N, NCOV), F32),
        pltpu.VMEM((N, LANES), F32),
        pltpu.SemaphoreType.DMA((CHUNKS + 3,)),
    ],
)
sum_cells = call(
    sum_kernel,
    "sum_cells",
    [pltpu.HBM(SUM_SHAPE, F32), pltpu.HBM(LIBRARY_SHAPE, F32)],
    [whole(PART_SHAPE)],
    24,
)
project = call(
    projection_kernel,
    "project",
    [pltpu.HBM(SQUARE, BF16)] * 3 + [pltpu.HBM(DOSAGE_SHAPE, BF16)],
    [whole(PART_SHAPE), whole(DOSAGE_SHAPE)],
    32,
)
associate = call(
    association_kernel,
    "associate",
    [jax.ShapeDtypeStruct((CT, OWN, WIN), F32)],
    [HBM, whole(LIBRARY_SHAPE), HBM, HBM, HBM, HBM, whole((OWN, WIN))],
    32,
    [
        pltpu.VMEM(SUM_SHAPE, F32),
        pltpu.VMEM(SQUARE, BF16),
        pltpu.VMEM(SQUARE, BF16),
        pltpu.VMEM(SQUARE, BF16),
        pltpu.VMEM(DOSAGE_SHAPE, BF16),
        pltpu.SemaphoreType.DMA((5,)),
    ],
)


def keep(array):
    return pltpu.with_memory_space_constraint(array, pltpu.HBM)


def per_device(counts, cell_donor, cell_type, covariates, dosage, windows):
    (parts,) = pack(
        keep(counts),
        keep(cell_donor.reshape(CHUNKS, LANES)),
        keep(cell_type.reshape(CHUNKS, LANES)),
        keep(covariates),
    )
    parts = lax.all_to_all(parts, ("cell", "donor"), 0, 0, tiled=True)
    sums, library = sum_cells(parts)
    library = lax.all_to_all(library, "gene", 0, 0, tiled=True)
    high, middle, low, dosage_half = project(parts, dosage)
    return associate(
        keep(sums),
        library,
        keep(high),
        keep(middle),
        keep(low),
        keep(dosage_half),
        windows,
    )[0]


def solution(mesh):
    in_specs = (
        P(("cell", "donor"), "gene"),
        P(("cell", "donor")),
        P(("cell", "donor")),
        P(("cell", "donor"), None),
        P("gene", None),
        P(("gene", "cell", "donor"), None),
    )
    out_specs = P(None, ("gene", "cell", "donor"), None)
    return jax.shard_map(
        per_device, mesh=mesh, in_specs=in_specs, out_specs=out_specs, check_vma=False
    )
```

```python
import math

import jax
import jax.numpy as jnp
from jax import lax
from jax.experimental import pallas as pl
from jax.experimental.pallas import tpu as pltpu
from jax.sharding import PartitionSpec as P

F32 = jnp.float32
BF16 = jnp.bfloat16
I32 = jnp.int32
HIGHEST = lax.Precision.HIGHEST

CT = 24
SUB = 8
PARTS = CT // SUB
NCOV = 50
ORDER = NCOV + 1
N = 8
PEERS = N * N
CELLS = 512
LANES = 128
CHUNKS = CELLS // LANES
GENES = 256
OWN = GENES // PEERS
DON_GRP = 64
DONORS = N * DON_GRP
SNPS = 1024
WIN = 1024
ROWS = 32
DONOR_ROW = CHUNKS * OWN
TYPE_ROW = DONOR_ROW + CHUNKS
TOTAL_ROW = TYPE_ROW + CHUNKS
COV_ROW = TOTAL_ROW + CHUNKS
KINDS = OWN + 2

NT = (((1,), (1,)), ((), ()))


def split3(value):
    high = value.astype(BF16)
    rest = value - high.astype(F32)
    middle = rest.astype(BF16)
    low = (rest - middle.astype(F32)).astype(BF16)
    return high, middle, low


def pack_kernel(
    counts_hbm, donor_hbm, type_hbm, cov_hbm, part_ref,
    counts_ref, donor_ref, type_ref, cov_ref, wide_ref, sems,
):
    copies = [
        pltpu.make_async_copy(
            counts_hbm.at[pl.ds(chunk * LANES, LANES)],
            counts_ref.at[pl.ds(chunk * LANES, LANES)],
            sems.at[chunk],
        )
        for chunk in range(CHUNKS)
    ]
    copies.append(pltpu.make_async_copy(donor_hbm, donor_ref, sems.at[CHUNKS]))
    copies.append(pltpu.make_async_copy(type_hbm, type_ref, sems.at[CHUNKS + 1]))
    copies.append(pltpu.make_async_copy(cov_hbm, cov_ref, sems.at[CHUNKS + 2]))
    for copy in copies:
        copy.start()
    totals = []
    for chunk in range(CHUNKS):
        copies[chunk].wait()
        turned = counts_ref[chunk * LANES : (chunk + 1) * LANES, :].astype(F32).T
        totals.append(jnp.sum(turned, axis=0, keepdims=True))
        for peer in range(PEERS):
            part_ref[peer, chunk * OWN : (chunk + 1) * OWN, :] = turned[
                peer * OWN : (peer + 1) * OWN
            ]
    for copy in copies[CHUNKS:]:
        copy.wait()
    wide_ref[...] = jnp.zeros_like(wide_ref)
    wide_ref[:, :NCOV] = cov_ref[...]
    wide = wide_ref[...]
    paired = wide[: N // 2] + pltpu.roll(wide, DON_GRP, 1)[N // 2 :]
    shared = jnp.concatenate(
        [donor_ref[...].astype(F32), type_ref[...].astype(F32), *totals, paired], axis=0
    )
    for peer in range(PEERS):
        part_ref[peer, DONOR_ROW:ROWS, :] = shared


def to_row(block):
    return jnp.concatenate([block[row : row + 1] for row in range(CHUNKS)], axis=1)


def sum_kernel(part_ref, sum_hbm, library_hbm, sum_ref, library_ref, sems):
    lane = lax.broadcasted_iota(I32, (KINDS * SUB, LANES), 1)
    place = lax.broadcasted_iota(I32, (PARTS * DON_GRP, CELLS), 0)
    place = place.astype(F32).astype(BF16)
    step = lax.broadcasted_iota(I32, (SUB, CELLS), 0)

    def one_block(block):
        donor = part_ref[block, DONOR_ROW:TYPE_ROW, :].astype(I32)
        kind = part_ref[block, TYPE_ROW:TOTAL_ROW, :].astype(I32)
        local = ((donor >> 6) << 3) + (donor & 7)
        column = jnp.where(kind >= 0, ((kind >> 3) << 6) + local, -1)
        column = to_row(column.astype(F32)).astype(BF16)
        one, zero = jnp.ones((), BF16), jnp.zeros((), BF16)
        onehot = jnp.where(place == column, one, zero)
        wanted = step == to_row(kind & 7)
        total = part_ref[block, TOTAL_ROW:COV_ROW, :]
        high = total.astype(BF16).astype(F32)
        values = [
            jnp.concatenate(
                [
                    part_ref[block, chunk * OWN + gene : chunk * OWN + gene + 1, :]
                    for chunk in range(CHUNKS)
                ],
                axis=1,
            )
            for gene in range(OWN)
        ]
        values += [to_row(high), to_row(total - high)]
        left = jnp.concatenate([jnp.where(wanted, value, 0.0) for value in values], axis=0)
        return lax.dot_general(onehot, left.astype(BF16), NT, preferred_element_type=F32)

    def one_pair(pair, carry):
        even, odd = one_block(2 * pair), one_block(2 * pair + 1)
        for cell in range(1, N):
            even = even + one_block(cell * N + 2 * pair)
            odd = odd + one_block(cell * N + 2 * pair + 1)
        even, odd = even.T, odd.T
        even_low, odd_low = even[:, :LANES], odd[:, :LANES]
        merged = [
            jnp.where(lane < DON_GRP, even_low, pltpu.roll(odd_low, DON_GRP, 1)),
            jnp.where(lane < DON_GRP, pltpu.roll(even_low, DON_GRP, 1), odd_low),
            jnp.concatenate([even[:, LANES:], odd[:, LANES:]], axis=1),
        ]
        span = pl.ds(pl.multiple_of(pair * LANES, LANES), LANES)
        for part, value in enumerate(merged):
            for gene in range(OWN):
                start = gene * CT + part * SUB
                sum_ref[start : start + SUB, span] = value[gene * SUB : (gene + 1) * SUB]
            library = value[OWN * SUB : (OWN + 1) * SUB] + value[(OWN + 1) * SUB :]
            library_ref[part * SUB : (part + 1) * SUB, span] = library
        return carry

    lax.fori_loop(0, N // 2, one_pair, 0)
    copies = [
        pltpu.make_async_copy(library_ref, library_hbm.at[peer], sems.at[peer])
        for peer in range(N)
    ]
    copies.append(pltpu.make_async_copy(sum_ref, sum_hbm, sems.at[N]))
    for copy in copies:
        copy.start()
    for copy in copies:
        copy.wait()


def projection_kernel(
    part_ref, dosage_ref, high_hbm, middle_hbm, low_hbm, dosage_hbm,
    high_ref, middle_ref, low_ref, half_ref, sems,
):
    half_ref[...] = dosage_ref[...].astype(F32).astype(BF16)
    copies = [pltpu.make_async_copy(half_ref, dosage_hbm, sems.at[0])]
    copies[0].start()
    lane = lax.broadcasted_iota(I32, (SUB, LANES), 1)
    first_half = lax.broadcasted_iota(I32, (SUB, LANES), 0) < N // 2
    tiles = []
    for block in range(PEERS):
        tile = part_ref[block, TOTAL_ROW:ROWS, :]
        rows = jnp.where(first_half, pltpu.roll(tile, N // 2, 0), pltpu.roll(tile, DON_GRP, 1))
        tiles.append(jnp.where(lane < NCOV, rows, jnp.where(lane == NCOV, 1.0, 0.0)))
    natural = jnp.concatenate(tiles, axis=0)
    grouped = jnp.concatenate(
        [tiles[cell * N + donor] for donor in range(N) for cell in range(N)], axis=0
    )
    turned = natural.T
    gram = lax.dot_general(turned, turned, NT, precision=HIGHEST, preferred_element_type=F32)
    rows = 56
    row_id = lax.broadcasted_iota(I32, (rows, LANES), 0)
    lane_id = lax.broadcasted_iota(I32, (rows, LANES), 1)
    work = jnp.where(lane_id < 64, gram[:rows], jnp.where(lane_id - 64 == row_id, 1.0, 0.0))
    row_col = lax.broadcasted_iota(I32, (rows, 1), 0)
    for panel in range(0, ORDER, SUB):
        members = range(panel, min(panel + SUB, ORDER))
        held = {
            column: jnp.broadcast_to(work[:, column : column + 1], (rows, LANES))
            for column in members
        }
        for column in members:
            mine = held[column]
            factor = jnp.where(row_id > column, mine, 0.0) * (1.0 / mine[column : column + 1])
            for later in range(column + 1, members.stop):
                held[later] = held[later] - factor * mine[later : later + 1]
            work = work - factor * work[column : column + 1]
    pivots = jnp.sum(jnp.where(lane_id == row_id, work, 0.0), axis=1, keepdims=True)
    scale = 1.0 / jnp.sqrt(jnp.where(row_col < ORDER, pivots, 1.0))
    inverse = pltpu.roll(work, 64, 1)
    inverse = jnp.where((lane_id < ORDER) & (row_id < ORDER), inverse * scale, 0.0)
    left = lax.dot_general(grouped, inverse, NT, precision=HIGHEST, preferred_element_type=F32)
    right = lax.dot_general(
        inverse, turned, (((1,), (0,)), ((), ())), precision=HIGHEST, preferred_element_type=F32
    )
    span = 128
    column = lax.broadcasted_iota(I32, (span, DONORS), 1)
    for start in range(0, DONORS, span):
        row = lax.broadcasted_iota(I32, (span, 1), 0) + start
        same = (((row >> 3) & 7) << 6) + ((row >> 6) << 3) + (row & 7) == column
        fitted = lax.dot_general(
            left[start : start + span],
            right,
            (((1,), (0,)), ((), ())),
            precision=HIGHEST,
            preferred_element_type=F32,
        )
        kept = jnp.where(same, 1.0, 0.0) - fitted
        targets = ((high_ref, high_hbm), (middle_ref, middle_hbm), (low_ref, low_hbm))
        for (held_ref, target), piece in zip(targets, split3(kept)):
            held_ref[start : start + span, :] = piece
            rows_here = pl.ds(start, span)
            copy = pltpu.make_async_copy(
                held_ref.at[rows_here], target.at[rows_here], sems.at[len(copies)]
            )
            copy.start()
            copies.append(copy)
    for copy in copies:
        copy.wait()


def association_kernel(
    sum_hbm, library_ref, high_hbm, middle_hbm, low_hbm, dosage_hbm, windows_ref, out_ref,
    sum_ref, high_ref, middle_ref, low_ref, dosage_ref, sems,
):
    pairs = (
        (sum_hbm, sum_ref),
        (high_hbm, high_ref),
        (middle_hbm, middle_ref),
        (low_hbm, low_ref),
        (dosage_hbm, dosage_ref),
    )
    copies = [
        pltpu.make_async_copy(source, target, sems.at[index])
        for index, (source, target) in enumerate(pairs)
    ]
    for copy in copies:
        copy.start()
    library = library_ref[0]
    for peer in range(1, N):
        library = library + library_ref[peer]
    library = library + 1.0
    copies[0].wait()
    expression = jnp.concatenate(
        [
            jnp.log2((sum_ref[gene * CT : (gene + 1) * CT] + 0.5) / library * 1000000.0)
            for gene in range(OWN)
        ],
        axis=0,
    )
    both = OWN * CT
    parts = jnp.concatenate(split3(expression), axis=0)
    plain = (((1,), (0,)), ((), ()))
    copies[1].wait()
    first = lax.dot_general(parts, high_ref[...], plain, preferred_element_type=F32)
    copies[2].wait()
    second = lax.dot_general(parts[: 2 * both], middle_ref[...], plain, preferred_element_type=F32)
    copies[3].wait()
    third = lax.dot_general(parts[:both], low_ref[...], plain, preferred_element_type=F32)
    residual = (
        (third + second[both:] + first[2 * both :]) + (second[:both] + first[both : 2 * both])
    ) + first[:both]
    upper_part = residual.astype(BF16)
    lower_part = (residual - upper_part.astype(F32)).astype(BF16)
    copies[4].wait()
    products = lax.dot_general(
        jnp.concatenate([upper_part, lower_part], axis=0),
        dosage_ref[...],
        NT,
        preferred_element_type=F32,
    )
    products = (products[:both] + products[both:]) * (1.0 / math.sqrt(DONORS))
    windows = windows_ref[...]
    lane = lax.broadcasted_iota(I32, (1, LANES), 1)
    for gene in range(OWN):
        first = jnp.where(lane == 0, windows[gene : gene + 1, :LANES], 0).astype(F32)
        start = jnp.sum(first).astype(I32) & (SNPS - 1)
        turned = pltpu.roll(
            products[gene * CT : (gene + 1) * CT], (SNPS - start) & (SNPS - 1), 1
        )
        live = windows[gene : gene + 1] >= 0
        out_ref[:, gene, :] = jnp.where(live, turned, 0.0)


MIB = 1024 * 1024
HBM = pl.BlockSpec(memory_space=pltpu.HBM)


VMEM = pl.BlockSpec(memory_space=pltpu.VMEM)


def call(kernel, name, outs, ins, limit, scratch=()):
    return pl.pallas_call(
        kernel,
        name=name,
        out_shape=[out for out, _ in outs],
        in_specs=ins,
        out_specs=[spec for _, spec in outs],
        scratch_shapes=scratch,
        compiler_params=pltpu.CompilerParams(vmem_limit_bytes=limit * MIB),
    )


PART_SHAPE = (PEERS, ROWS, LANES)
LIBRARY_SHAPE = (N, CT, DONORS)
SUM_SHAPE = (OWN * CT, DONORS)
SQUARE = (DONORS, DONORS)
DOSAGE_SHAPE = (SNPS, DONORS)

pack = call(
    pack_kernel,
    "pack",
    [(jax.ShapeDtypeStruct(PART_SHAPE, F32), VMEM)],
    [HBM] * 4,
    8,
    [
        pltpu.VMEM((CELLS, GENES), I32),
        pltpu.VMEM((CHUNKS, LANES), I32),
        pltpu.VMEM((CHUNKS, LANES), I32),
        pltpu.VMEM((N, NCOV), F32),
        pltpu.VMEM((N, LANES), F32),
        pltpu.SemaphoreType.DMA((CHUNKS + 3,)),
    ],
)
sum_cells = call(
    sum_kernel,
    "sum_cells",
    [(pltpu.HBM(SUM_SHAPE, F32), HBM), (pltpu.HBM(LIBRARY_SHAPE, F32), HBM)],
    [VMEM],
    16,
    [
        pltpu.VMEM(SUM_SHAPE, F32),
        pltpu.VMEM((CT, DONORS), F32),
        pltpu.SemaphoreType.DMA((N + 1,)),
    ],
)
MATRICES = (SQUARE, SQUARE, SQUARE, DOSAGE_SHAPE)
project = call(
    projection_kernel,
    "project",
    [(pltpu.HBM(dims, BF16), HBM) for dims in MATRICES],
    [VMEM, VMEM],
    16,
    [pltpu.VMEM(dims, BF16) for dims in MATRICES] + [pltpu.SemaphoreType.DMA((13,))],
)
associate = call(
    association_kernel,
    "associate",
    [(jax.ShapeDtypeStruct((CT, OWN, WIN), F32), VMEM)],
    [HBM, VMEM, HBM, HBM, HBM, HBM, VMEM],
    16,
    [pltpu.VMEM(SUM_SHAPE, F32)]
    + [pltpu.VMEM(dims, BF16) for dims in MATRICES]
    + [pltpu.SemaphoreType.DMA((5,))],
)


def keep(array):
    return pltpu.with_memory_space_constraint(array, pltpu.HBM)


def per_device(counts, cell_donor, cell_type, covariates, dosage, windows):
    (parts,) = pack(
        keep(counts),
        keep(cell_donor.reshape(CHUNKS, LANES)),
        keep(cell_type.reshape(CHUNKS, LANES)),
        keep(covariates),
    )
    parts = lax.all_to_all(parts, ("cell", "donor"), 0, 0, tiled=True)
    sums, library = sum_cells(parts)
    library = lax.all_to_all(library, "gene", 0, 0, tiled=True)
    high, middle, low, dosage_half = project(parts, dosage)
    return associate(
        keep(sums),
        library,
        keep(high),
        keep(middle),
        keep(low),
        keep(dosage_half),
        windows,
    )[0]


def solution(mesh):
    in_specs = (
        P(("cell", "donor"), "gene"),
        P(("cell", "donor")),
        P(("cell", "donor")),
        P(("cell", "donor"), None),
        P("gene", None),
        P(("gene", "cell", "donor"), None),
    )
    out_specs = P(None, ("gene", "cell", "donor"), None)
    return jax.shard_map(
        per_device, mesh=mesh, in_specs=in_specs, out_specs=out_specs, check_vma=False
    )
```

```python
import math

import jax
import jax.numpy as jnp
from jax import lax
from jax.experimental import pallas as pl
from jax.experimental.pallas import tpu as pltpu
from jax.sharding import PartitionSpec as P

F32 = jnp.float32
BF16 = jnp.bfloat16
I32 = jnp.int32
HIGHEST = lax.Precision.HIGHEST

CT = 24
HALF = CT // 2
SUB = 8
NCOV = 50
ORDER = NCOV + 1
ORDER_ROWS = 56
N = 8
CELLS = 512
LANES = 128
CHUNKS = CELLS // LANES
GENES = 256
GENE_PART = GENES // N
OWN = GENE_PART // N
DON_GRP = 64
DONORS = N * DON_GRP
SNPS = 1024
WIN = 1024
DONOR_ROW = CHUNKS * GENE_PART
TYPE_ROW = DONOR_ROW + CHUNKS
TOTAL_ROW = TYPE_ROW + CHUNKS
COV_ROW = TOTAL_ROW + CHUNKS
PART_ROWS = COV_ROW + N // 2
SUM_ROWS = HALF * GENE_PART
LIB_ROWS = 16
EXPR_ROWS = HALF * OWN
SEND_ROWS = EXPR_ROWS + N * N // 2

NT = (((1,), (1,)), ((), ()))
PLAIN = (((1,), (0,)), ((), ()))


def pack_kernel(
    counts_hbm, donor_hbm, type_hbm, cov_hbm, part_ref,
    counts_ref, donor_ref, type_ref, cov_ref, wide_ref, sems,
):
    copies = [
        pltpu.make_async_copy(
            counts_hbm.at[pl.ds(chunk * LANES, LANES)],
            counts_ref.at[pl.ds(chunk * LANES, LANES)],
            sems.at[chunk],
        )
        for chunk in range(CHUNKS)
    ]
    copies.append(pltpu.make_async_copy(donor_hbm, donor_ref, sems.at[CHUNKS]))
    copies.append(pltpu.make_async_copy(type_hbm, type_ref, sems.at[CHUNKS + 1]))
    copies.append(pltpu.make_async_copy(cov_hbm, cov_ref, sems.at[CHUNKS + 2]))
    for copy in copies:
        copy.start()
    totals = []
    for chunk in range(CHUNKS):
        copies[chunk].wait()
        turned = counts_ref[chunk * LANES : (chunk + 1) * LANES, :].astype(F32).T
        totals.append(jnp.sum(turned, axis=0, keepdims=True))
        for peer in range(N):
            part_ref[peer, chunk * GENE_PART : (chunk + 1) * GENE_PART, :] = turned[
                peer * GENE_PART : (peer + 1) * GENE_PART
            ]
    for copy in copies[CHUNKS:]:
        copy.wait()
    wide_ref[...] = jnp.zeros_like(wide_ref)
    wide_ref[:, :NCOV] = cov_ref[...]
    wide = wide_ref[...]
    paired = wide[: N // 2] + pltpu.roll(wide, DON_GRP, 1)[N // 2 :]
    shared = jnp.concatenate(
        [donor_ref[...].astype(F32), type_ref[...].astype(F32), *totals, paired], axis=0
    )
    for peer in range(N):
        part_ref[peer, DONOR_ROW:PART_ROWS, :] = shared


def to_row(block):
    return jnp.concatenate([block[row : row + 1] for row in range(CHUNKS)], axis=1)


def read_labels(part_ref, block):
    donor = part_ref[block, DONOR_ROW:TYPE_ROW, :].astype(I32)
    kind = part_ref[block, TYPE_ROW:TOTAL_ROW, :].astype(I32)
    local = ((donor >> 6) << 3) + (donor & 7)
    upper = kind >= HALF
    column = jnp.where(kind >= 0, jnp.where(upper, local + DON_GRP, local), -1)
    place = lax.broadcasted_iota(I32, (LANES, CELLS), 0)
    onehot = jnp.where(place == to_row(column), 1.0, 0.0).astype(BF16)
    return onehot, to_row(jnp.where(upper, kind - HALF, kind))


def library_kernel(part_ref, library_hbm, library_ref, sems):
    number = lax.broadcasted_iota(I32, (LIB_ROWS, CELLS), 0)
    summed = jnp.zeros((2 * LIB_ROWS, LANES), F32)
    for block in range(N):
        onehot, step = read_labels(part_ref, block)
        total = part_ref[block, TOTAL_ROW:COV_ROW, :]
        high = total.astype(BF16).astype(F32)
        left = jnp.concatenate(
            [jnp.where(number == step, to_row(value), 0.0) for value in (high, total - high)],
            axis=0,
        )
        summed = summed + lax.dot_general(
            left.astype(BF16), onehot, NT, preferred_element_type=F32
        )
    library_ref[...] = summed[:LIB_ROWS] + summed[LIB_ROWS:]
    copies = [
        pltpu.make_async_copy(library_ref, library_hbm.at[peer], sems.at[peer])
        for peer in range(N)
    ]
    for copy in copies:
        copy.start()
    for copy in copies:
        copy.wait()


def sum_kernel(part_ref, sum_hbm, sum_ref, sem):
    sum_ref[...] = jnp.zeros_like(sum_ref)

    def one_block(block, carry):
        onehot, step = read_labels(part_ref, block)
        counts = jnp.concatenate(
            [
                part_ref[block, chunk * GENE_PART : (chunk + 1) * GENE_PART, :]
                for chunk in range(CHUNKS)
            ],
            axis=1,
        )
        step = jnp.broadcast_to(step, (GENE_PART, CELLS))
        left = jnp.concatenate(
            [jnp.where(step == number, counts, 0.0).astype(BF16) for number in range(HALF)],
            axis=0,
        )
        sum_ref[...] += lax.dot_general(left, onehot, NT, preferred_element_type=F32)
        return carry

    lax.fori_loop(0, N, one_block, 0)
    copy = pltpu.make_async_copy(sum_ref, sum_hbm, sem)
    copy.start()
    copy.wait()


def expression_kernel(part_ref, sum_hbm, library_ref, out_ref, sum_ref, sem):
    copy = pltpu.make_async_copy(sum_hbm, sum_ref, sem)
    copy.start()
    for cell in range(N):
        row = EXPR_ROWS + cell * (N // 2)
        packed = part_ref[cell, COV_ROW:PART_ROWS, :]
        for peer in range(N):
            out_ref[peer, row : row + N // 2, :] = packed
    library = library_ref[0]
    for peer in range(1, N):
        library = library + library_ref[peer]
    library = library + 1.0
    copy.wait()
    for step in range(HALF):
        summed = sum_ref[step * GENE_PART : (step + 1) * GENE_PART, :]
        expression = jnp.log2((summed + 0.5) / library[step : step + 1] * 1000000.0)
        for peer in range(N):
            out_ref[peer, step * OWN : (step + 1) * OWN, :] = expression[
                peer * OWN : (peer + 1) * OWN
            ]


def dosage_kernel(dosage_ref, out_hbm, out_ref, sem):
    row = lax.broadcasted_iota(I32, (DONORS, DONORS), 0)
    place = lax.broadcasted_iota(I32, (1, DONORS), 1)
    source = (((place >> 3) & 7) << 6) + ((place >> 6) << 3) + (place & 7)
    order = jnp.where(row == source, 1.0, 0.0).astype(BF16)
    span = 256
    for start in range(0, SNPS, span):
        half = dosage_ref[start : start + span, :].astype(F32).astype(BF16)
        moved = lax.dot_general(half, order, PLAIN, preferred_element_type=F32)
        out_ref[start : start + span, :] = moved.astype(BF16)
    copy = pltpu.make_async_copy(out_ref, out_hbm, sem)
    copy.start()
    copy.wait()


def association_kernel(
    recv_ref, dosage_hbm, windows_ref, out_ref, dosage_ref, expression_ref, sem
):
    copy = pltpu.make_async_copy(dosage_hbm, dosage_ref, sem)
    copy.start()
    lane = lax.broadcasted_iota(I32, (SUB, LANES), 1)
    first_half = lax.broadcasted_iota(I32, (SUB, LANES), 0) < N // 2
    tiles = []
    for donor in range(N):
        for pair in range(N // 2):
            row = EXPR_ROWS + pair * SUB
            tile = recv_ref[donor, row : row + SUB, :]
            other = pltpu.roll(tile, DON_GRP, 1)
            tiles.append(jnp.where(first_half, tile, pltpu.roll(other, N // 2, 0)))
            tiles.append(jnp.where(first_half, pltpu.roll(tile, N // 2, 0), other))
    ends = jnp.where(lane == NCOV, 1.0, 0.0)
    design = jnp.concatenate([jnp.where(lane < NCOV, tile, ends) for tile in tiles], axis=0)
    turned = design.T
    gram = lax.dot_general(turned, turned, NT, precision=HIGHEST, preferred_element_type=F32)
    rows = ORDER_ROWS
    row_id = lax.broadcasted_iota(I32, (rows, LANES), 0)
    lane_id = lax.broadcasted_iota(I32, (rows, LANES), 1)
    row_col = lax.broadcasted_iota(I32, (rows, 1), 0)
    work = jnp.where(lane_id < 64, gram[:rows], jnp.where(lane_id - 64 == row_id, 1.0, 0.0))
    for panel in range(0, ORDER, SUB):
        members = range(panel, min(panel + SUB, ORDER))
        held = {
            column: jnp.broadcast_to(work[:, column : column + 1], (rows, LANES))
            for column in members
        }
        for column in members:
            mine = held[column]
            factor = jnp.where(row_id > column, mine, 0.0) * (1.0 / mine[column : column + 1])
            for later in range(column + 1, members.stop):
                held[later] = held[later] - factor * mine[later : later + 1]
            work = work - factor * work[column : column + 1]
    pivots = jnp.sum(jnp.where(lane_id == row_id, work, 0.0), axis=1, keepdims=True)
    scale = 1.0 / jnp.sqrt(jnp.where(row_col < ORDER, pivots, 1.0))
    inverse = pltpu.roll(work, 64, 1)
    inverse = jnp.where((lane_id < ORDER) & (row_id < ORDER), inverse * scale, 0.0)
    basis = lax.dot_general(inverse, turned, PLAIN, precision=HIGHEST, preferred_element_type=F32)
    wide_lane = lax.broadcasted_iota(I32, (EXPR_ROWS, LANES), 1)
    for pair in range(N // 2):
        one, two = recv_ref[2 * pair, :EXPR_ROWS, :], recv_ref[2 * pair + 1, :EXPR_ROWS, :]
        expression_ref[pair, :EXPR_ROWS, :] = jnp.where(
            wide_lane < DON_GRP, one, pltpu.roll(two, DON_GRP, 1)
        )
        expression_ref[pair, EXPR_ROWS:, :] = jnp.where(
            wide_lane < DON_GRP, pltpu.roll(one, DON_GRP, 1), two
        )
    expression = jnp.concatenate(
        [
            jnp.concatenate(
                [
                    expression_ref[pair, pl.ds(gene, CT, stride=OWN), :]
                    for gene in range(OWN)
                ],
                axis=0,
            )
            for pair in range(N // 2)
        ],
        axis=1,
    )
    fit = lax.dot_general(expression, basis, NT, precision=HIGHEST, preferred_element_type=F32)
    residual = expression - lax.dot_general(
        fit, basis, PLAIN, precision=HIGHEST, preferred_element_type=F32
    )
    upper_part = residual.astype(BF16)
    lower_part = (residual - upper_part.astype(F32)).astype(BF16)
    copy.wait()
    products = lax.dot_general(
        jnp.concatenate([upper_part, lower_part], axis=0),
        dosage_ref[...],
        NT,
        preferred_element_type=F32,
    )
    both = OWN * CT
    products = (products[:both] + products[both:]) * (1.0 / math.sqrt(DONORS))
    windows = windows_ref[...]
    first_lane = lax.broadcasted_iota(I32, (1, LANES), 1) == 0
    for gene in range(OWN):
        first = jnp.where(first_lane, windows[gene : gene + 1, :LANES], 0).astype(F32)
        start = jnp.sum(first).astype(I32) & (SNPS - 1)
        turned_back = pltpu.roll(
            products[gene * CT : (gene + 1) * CT], (SNPS - start) & (SNPS - 1), 1
        )
        live = windows[gene : gene + 1] >= 0
        out_ref[:, gene, :] = jnp.where(live, turned_back, 0.0)


MIB = 1024 * 1024
HBM = pl.BlockSpec(memory_space=pltpu.HBM)


VMEM = pl.BlockSpec(memory_space=pltpu.VMEM)


def call(kernel, name, outs, ins, limit, scratch=()):
    return pl.pallas_call(
        kernel,
        name=name,
        out_shape=[out for out, _ in outs],
        in_specs=ins,
        out_specs=[spec for _, spec in outs],
        scratch_shapes=scratch,
        compiler_params=pltpu.CompilerParams(vmem_limit_bytes=limit * MIB),
    )


PART_SHAPE = (N, PART_ROWS, LANES)
SUM_SHAPE = (SUM_ROWS, LANES)
LIBRARY_SHAPE = (N, LIB_ROWS, LANES)
SEND_SHAPE = (N, SEND_ROWS, LANES)
DOSAGE_SHAPE = (SNPS, DONORS)
DMA = pltpu.SemaphoreType.DMA

pack = call(
    pack_kernel,
    "pack",
    [(jax.ShapeDtypeStruct(PART_SHAPE, F32), VMEM)],
    [HBM] * 4,
    8,
    [
        pltpu.VMEM((CELLS, GENES), I32),
        pltpu.VMEM((CHUNKS, LANES), I32),
        pltpu.VMEM((CHUNKS, LANES), I32),
        pltpu.VMEM((N, NCOV), F32),
        pltpu.VMEM((N, LANES), F32),
        DMA((CHUNKS + 3,)),
    ],
)
sum_library = call(
    library_kernel,
    "sum_library",
    [(pltpu.HBM(LIBRARY_SHAPE, F32), HBM)],
    [VMEM],
    8,
    [pltpu.VMEM(LIBRARY_SHAPE[1:], F32), DMA((N,))],
)
sum_cells = call(
    sum_kernel,
    "sum_cells",
    [(pltpu.HBM(SUM_SHAPE, F32), HBM)],
    [VMEM],
    16,
    [pltpu.VMEM(SUM_SHAPE, F32), DMA],
)
express = call(
    expression_kernel,
    "express",
    [(jax.ShapeDtypeStruct(SEND_SHAPE, F32), VMEM)],
    [VMEM, HBM, VMEM],
    8,
    [pltpu.VMEM(SUM_SHAPE, F32), DMA],
)
order_dosage = call(
    dosage_kernel,
    "order_dosage",
    [(pltpu.HBM(DOSAGE_SHAPE, BF16), HBM)],
    [VMEM],
    16,
    [pltpu.VMEM(DOSAGE_SHAPE, BF16), DMA],
)
associate = call(
    association_kernel,
    "associate",
    [(jax.ShapeDtypeStruct((CT, OWN, WIN), F32), VMEM)],
    [VMEM, HBM, VMEM],
    16,
    [pltpu.VMEM(DOSAGE_SHAPE, BF16), pltpu.VMEM((N // 2, OWN * CT, LANES), F32), DMA],
)


def keep(array):
    return pltpu.with_memory_space_constraint(array, pltpu.HBM)


def per_device(counts, cell_donor, cell_type, covariates, dosage, windows):
    (parts,) = pack(
        keep(counts),
        keep(cell_donor.reshape(CHUNKS, LANES)),
        keep(cell_type.reshape(CHUNKS, LANES)),
        keep(covariates),
    )
    parts = lax.all_to_all(parts, "cell", 0, 0, tiled=True)
    (ordered,) = order_dosage(dosage)
    (library,) = sum_library(parts)
    library = lax.all_to_all(library, "gene", 0, 0, tiled=True)
    (sums,) = sum_cells(parts)
    (sent,) = express(parts, keep(sums), library)
    sent = lax.all_to_all(sent, "donor", 0, 0, tiled=True)
    return associate(sent, keep(ordered), windows)[0]


def solution(mesh):
    in_specs = (
        P(("cell", "donor"), "gene"),
        P(("cell", "donor")),
        P(("cell", "donor")),
        P(("cell", "donor"), None),
        P("gene", None),
        P(("gene", "cell", "donor"), None),
    )
    out_specs = P(None, ("gene", "cell", "donor"), None)
    return jax.shard_map(
        per_device, mesh=mesh, in_specs=in_specs, out_specs=out_specs, check_vma=False
    )
```

```python
import math

import jax
import jax.numpy as jnp
from jax import lax
from jax.experimental import pallas as pl
from jax.experimental.pallas import tpu as pltpu
from jax.sharding import PartitionSpec as P

F32 = jnp.float32
BF16 = jnp.bfloat16
I32 = jnp.int32
HIGHEST = lax.Precision.HIGHEST

CT = 24
HALF = CT // 2
SUB = 8
NCOV = 50
ORDER = NCOV + 1
ORDER_ROWS = 56
N = 8
CELLS = 512
LANES = 128
CHUNKS = CELLS // LANES
GENES = 256
GENE_PART = GENES // N
OWN = GENE_PART // N
DON_GRP = 64
DONORS = N * DON_GRP
SNPS = 1024
WIN = 1024
DONOR_ROW = CHUNKS * GENE_PART
TYPE_ROW = DONOR_ROW + CHUNKS
TOTAL_ROW = TYPE_ROW + CHUNKS
COV_ROW = TOTAL_ROW + CHUNKS
PART_ROWS = COV_ROW + N // 2
SUM_ROWS = HALF * GENE_PART
LIB_ROWS = 16
EXPR_ROWS = HALF * OWN
SEND_ROWS = EXPR_ROWS + DON_GRP // 2

NT = (((1,), (1,)), ((), ()))
PLAIN = (((1,), (0,)), ((), ()))


def pack_kernel(
    counts_hbm, donor_hbm, type_hbm, cov_hbm, part_ref,
    counts_ref, donor_ref, type_ref, cov_ref, wide_ref, sems,
):
    copies = [
        pltpu.make_async_copy(
            counts_hbm.at[pl.ds(chunk * LANES, LANES)],
            counts_ref.at[pl.ds(chunk * LANES, LANES)],
            sems.at[chunk],
        )
        for chunk in range(CHUNKS)
    ]
    copies.append(pltpu.make_async_copy(donor_hbm, donor_ref, sems.at[CHUNKS]))
    copies.append(pltpu.make_async_copy(type_hbm, type_ref, sems.at[CHUNKS + 1]))
    copies.append(pltpu.make_async_copy(cov_hbm, cov_ref, sems.at[CHUNKS + 2]))
    for copy in copies:
        copy.start()
    totals = []
    for chunk in range(CHUNKS):
        copies[chunk].wait()
        turned = counts_ref[chunk * LANES : (chunk + 1) * LANES, :].astype(F32).T
        totals.append(jnp.sum(turned, axis=0, keepdims=True))
        for peer in range(N):
            part_ref[peer, chunk * GENE_PART : (chunk + 1) * GENE_PART, :] = turned[
                peer * GENE_PART : (peer + 1) * GENE_PART
            ]
    for copy in copies[CHUNKS:]:
        copy.wait()
    wide_ref[...] = jnp.zeros_like(wide_ref)
    wide_ref[:, :NCOV] = cov_ref[...]
    wide = wide_ref[...]
    paired = wide[: N // 2] + pltpu.roll(wide, DON_GRP, 1)[N // 2 :]
    shared = jnp.concatenate(
        [donor_ref[...].astype(F32), type_ref[...].astype(F32), *totals, paired], axis=0
    )
    for peer in range(N):
        part_ref[peer, DONOR_ROW:PART_ROWS, :] = shared


def to_row(block):
    return jnp.concatenate([block[row : row + 1] for row in range(CHUNKS)], axis=1)


def read_labels(part_ref, block):
    donor = part_ref[block, DONOR_ROW:TYPE_ROW, :].astype(I32)
    kind = part_ref[block, TYPE_ROW:TOTAL_ROW, :].astype(I32)
    local = ((donor >> 6) << 3) + (donor & 7)
    upper = kind >= HALF
    column = jnp.where(kind >= 0, jnp.where(upper, local + DON_GRP, local), -1)
    place = lax.broadcasted_iota(I32, (LANES, CELLS), 0)
    onehot = jnp.where(place == to_row(column), 1.0, 0.0).astype(BF16)
    return onehot, to_row(jnp.where(upper, kind - HALF, kind))


def library_kernel(part_ref, library_hbm, library_ref, sems):
    number = lax.broadcasted_iota(I32, (LIB_ROWS, CELLS), 0)
    summed = jnp.zeros((2 * LIB_ROWS, LANES), F32)
    for block in range(N):
        onehot, step = read_labels(part_ref, block)
        total = part_ref[block, TOTAL_ROW:COV_ROW, :]
        high = total.astype(BF16).astype(F32)
        left = jnp.concatenate(
            [jnp.where(number == step, to_row(value), 0.0) for value in (high, total - high)],
            axis=0,
        )
        summed = summed + lax.dot_general(
            left.astype(BF16), onehot, NT, preferred_element_type=F32
        )
    library_ref[...] = summed[:LIB_ROWS] + summed[LIB_ROWS:]
    copies = [
        pltpu.make_async_copy(library_ref, library_hbm.at[peer], sems.at[peer])
        for peer in range(N)
    ]
    for copy in copies:
        copy.start()
    for copy in copies:
        copy.wait()


def sum_kernel(part_ref, out_hbm, sum_ref, out_ref, sems):
    lane = lax.broadcasted_iota(I32, (SUB, LANES), 1)
    first_half = lax.broadcasted_iota(I32, (SUB, LANES), 0) < N // 2
    tiles = []
    for cell in range(N):
        tile = part_ref[cell, TOTAL_ROW:PART_ROWS, :]
        tile = jnp.where(first_half, pltpu.roll(tile, N // 2, 0), pltpu.roll(tile, DON_GRP, 1))
        tiles.append(jnp.where(lane < NCOV, tile, jnp.where(lane == NCOV, 1.0, 0.0)))
    tiles.append(jnp.zeros((DON_GRP, LANES), F32))
    turned = jnp.concatenate(tiles, axis=0).T
    design = turned[: DON_GRP // 2] + pltpu.roll(turned[DON_GRP // 2 : DON_GRP], DON_GRP, 1)
    for peer in range(N):
        out_ref[peer, EXPR_ROWS:, :] = design

    def one_block(block):
        onehot, step = read_labels(part_ref, block)
        counts = jnp.concatenate(
            [
                part_ref[block, chunk * GENE_PART : (chunk + 1) * GENE_PART, :]
                for chunk in range(CHUNKS)
            ],
            axis=1,
        )
        step = jnp.broadcast_to(step, (GENE_PART, CELLS))
        left = jnp.concatenate(
            [jnp.where(step == number, counts, 0.0).astype(BF16) for number in range(HALF)],
            axis=0,
        )
        return lax.dot_general(left, onehot, NT, preferred_element_type=F32)

    for block in range(0, N, 2):
        added = one_block(block) + one_block(block + 1)
        if block == 0:
            sum_ref[...] = added
        else:
            sum_ref[...] += added
    for step in range(HALF):
        logs = jnp.log2(sum_ref[step * GENE_PART : (step + 1) * GENE_PART, :] + 0.5)
        for peer in range(N):
            out_ref[peer, step * OWN : (step + 1) * OWN, :] = logs[peer * OWN : (peer + 1) * OWN]
    copy_all([(out_ref.at[peer], out_hbm.at[peer]) for peer in range(N)], sems)


def copy_all(pairs, sems):
    copies = [
        pltpu.make_async_copy(source, target, sems.at[index])
        for index, (source, target) in enumerate(pairs)
    ]
    for copy in copies:
        copy.start()
    for copy in copies:
        copy.wait()


def expression_kernel(sent_hbm, library_ref, out_hbm, sent_ref, in_sems, out_sems):
    logs = pl.ds(0, EXPR_ROWS)
    arrivals = [
        pltpu.make_async_copy(sent_hbm.at[peer, logs], sent_ref.at[peer], in_sems.at[peer])
        for peer in range(N)
    ]
    for copy in arrivals:
        copy.start()
    library = library_ref[0]
    for peer in range(1, N):
        library = library + library_ref[peer]
    shift = math.log2(1000000.0) - jnp.log2(library + 1.0)
    shift = jnp.concatenate(
        [jnp.broadcast_to(shift[step : step + 1], (OWN, LANES)) for step in range(HALF)], axis=0
    )
    departures = []
    for peer in range(N):
        arrivals[peer].wait()
        sent_ref[peer] += shift
        departures.append(
            pltpu.make_async_copy(sent_ref.at[peer], out_hbm.at[peer, logs], out_sems.at[peer])
        )
        departures[peer].start()
    for copy in departures:
        copy.wait()


def dosage_kernel(dosage_ref, out_hbm, out_ref, sem):
    place = lax.broadcasted_iota(I32, (DONORS, 1), 0)
    column = lax.broadcasted_iota(I32, (DONORS, DONORS), 1)
    source = (((place >> 3) & 7) << 6) + ((place >> 6) << 3) + (place & 7)
    order = jnp.where(column == source, 1.0, 0.0).astype(BF16)
    span = 256
    for start in range(0, SNPS, span):
        half = dosage_ref[start : start + span, :].astype(F32).astype(BF16)
        moved = lax.dot_general(order, half, NT, preferred_element_type=F32)
        out_ref[:, start : start + span] = moved.astype(BF16)
    copy = pltpu.make_async_copy(out_ref, out_hbm, sem)
    copy.start()
    copy.wait()


def association_kernel(
    recv_ref, dosage_hbm, windows_ref, out_ref, dosage_ref, expression_ref, sem
):
    copy = pltpu.make_async_copy(dosage_hbm, dosage_ref, sem)
    copy.start()
    half_rows = DON_GRP // 2
    lane = lax.broadcasted_iota(I32, (half_rows, LANES), 1)
    lower, upper = [], []
    for pair in range(N // 2):
        one, two = recv_ref[2 * pair, EXPR_ROWS:, :], recv_ref[2 * pair + 1, EXPR_ROWS:, :]
        lower.append(jnp.where(lane < DON_GRP, one, pltpu.roll(two, DON_GRP, 1)))
        upper.append(jnp.where(lane < DON_GRP, pltpu.roll(one, DON_GRP, 1), two))
    turned = jnp.concatenate(
        [jnp.concatenate(lower, axis=1), jnp.concatenate(upper, axis=1)], axis=0
    )
    padded = jnp.concatenate([turned, jnp.zeros_like(turned)], axis=0)
    wide_lane = lax.broadcasted_iota(I32, (EXPR_ROWS, LANES), 1)
    for pair in range(N // 2):
        one, two = recv_ref[2 * pair, :EXPR_ROWS, :], recv_ref[2 * pair + 1, :EXPR_ROWS, :]
        expression_ref[pair, :EXPR_ROWS, :] = jnp.where(
            wide_lane < DON_GRP, one, pltpu.roll(two, DON_GRP, 1)
        )
        expression_ref[pair, EXPR_ROWS:, :] = jnp.where(
            wide_lane < DON_GRP, pltpu.roll(one, DON_GRP, 1), two
        )
    expression = jnp.concatenate(
        [
            jnp.concatenate(
                [
                    expression_ref[pair, pl.ds(gene, CT, stride=OWN), :]
                    for gene in range(OWN)
                ],
                axis=0,
            )
            for pair in range(N // 2)
        ],
        axis=1,
    )
    cross = lax.dot_general(expression, padded, NT, precision=HIGHEST, preferred_element_type=F32)
    gram = lax.dot_general(turned, padded, NT, precision=HIGHEST, preferred_element_type=F32)
    rows = ORDER_ROWS
    row_id = lax.broadcasted_iota(I32, (rows, LANES), 0)
    lane_id = lax.broadcasted_iota(I32, (rows, LANES), 1)
    row_col = lax.broadcasted_iota(I32, (rows, 1), 0)
    work = jnp.where(lane_id < 64, gram[:rows], jnp.where(lane_id - 64 == row_id, 1.0, 0.0))
    for panel in range(0, ORDER, SUB):
        members = range(panel, min(panel + SUB, ORDER))
        held = {
            column: jnp.broadcast_to(work[:, column : column + 1], (rows, LANES))
            for column in members
        }
        for column in members:
            mine = held[column]
            factor = jnp.where(row_id > column, mine, 0.0) * (1.0 / mine[column : column + 1])
            for later in range(column + 1, members.stop):
                held[later] = held[later] - factor * mine[later : later + 1]
            work = work - factor * work[column : column + 1]
    pivots = jnp.sum(jnp.where(lane_id == row_id, work, 0.0), axis=1, keepdims=True)
    scale = 1.0 / jnp.sqrt(jnp.where(row_col < ORDER, pivots, 1.0))
    inverse = pltpu.roll(work, 64, 1)
    inverse = jnp.where((lane_id < ORDER) & (row_id < ORDER), inverse * scale, 0.0)
    half_way = lax.dot_general(cross, inverse, NT, precision=HIGHEST, preferred_element_type=F32)
    coefficients = lax.dot_general(
        half_way, inverse, PLAIN, precision=HIGHEST, preferred_element_type=F32
    )
    residual = expression - lax.dot_general(
        coefficients, padded, PLAIN, precision=HIGHEST, preferred_element_type=F32
    )
    upper_part = residual.astype(BF16)
    lower_part = (residual - upper_part.astype(F32)).astype(BF16)
    copy.wait()
    products = lax.dot_general(
        jnp.concatenate([upper_part, lower_part], axis=0),
        dosage_ref[...],
        PLAIN,
        preferred_element_type=F32,
    )
    both = OWN * CT
    products = (products[:both] + products[both:]) * (1.0 / math.sqrt(DONORS))
    windows = windows_ref[...]
    first_lane = lax.broadcasted_iota(I32, (1, LANES), 1) == 0
    for gene in range(OWN):
        first = jnp.where(first_lane, windows[gene : gene + 1, :LANES], 0).astype(F32)
        start = jnp.sum(first).astype(I32) & (SNPS - 1)
        turned_back = pltpu.roll(
            products[gene * CT : (gene + 1) * CT], (SNPS - start) & (SNPS - 1), 1
        )
        live = windows[gene : gene + 1] >= 0
        out_ref[:, gene, :] = jnp.where(live, turned_back, 0.0)


MIB = 1024 * 1024
HBM = pl.BlockSpec(memory_space=pltpu.HBM)


VMEM = pl.BlockSpec(memory_space=pltpu.VMEM)


def call(kernel, name, outs, ins, limit, scratch=(), aliases=None):
    return pl.pallas_call(
        kernel,
        name=name,
        out_shape=[out for out, _ in outs],
        in_specs=ins,
        out_specs=[spec for _, spec in outs],
        scratch_shapes=scratch,
        input_output_aliases=aliases or {},
        compiler_params=pltpu.CompilerParams(vmem_limit_bytes=limit * MIB),
    )


PART_SHAPE = (N, PART_ROWS, LANES)
SUM_SHAPE = (SUM_ROWS, LANES)
LIBRARY_SHAPE = (N, LIB_ROWS, LANES)
SEND_SHAPE = (N, SEND_ROWS, LANES)
DOSAGE_SHAPE = (DONORS, SNPS)
DMA = pltpu.SemaphoreType.DMA

pack = call(
    pack_kernel,
    "pack",
    [(jax.ShapeDtypeStruct(PART_SHAPE, F32), VMEM)],
    [HBM] * 4,
    8,
    [
        pltpu.VMEM((CELLS, GENES), I32),
        pltpu.VMEM((CHUNKS, LANES), I32),
        pltpu.VMEM((CHUNKS, LANES), I32),
        pltpu.VMEM((N, NCOV), F32),
        pltpu.VMEM((N, LANES), F32),
        DMA((CHUNKS + 3,)),
    ],
)
sum_library = call(
    library_kernel,
    "sum_library",
    [(pltpu.HBM(LIBRARY_SHAPE, F32), HBM)],
    [VMEM],
    8,
    [pltpu.VMEM(LIBRARY_SHAPE[1:], F32), DMA((N,))],
)
sum_cells = call(
    sum_kernel,
    "sum_cells",
    [(pltpu.HBM(SEND_SHAPE, F32), HBM)],
    [VMEM],
    16,
    [pltpu.VMEM(SUM_SHAPE, F32), pltpu.VMEM(SEND_SHAPE, F32), DMA((N,))],
)
express = call(
    expression_kernel,
    "express",
    [(pltpu.HBM(SEND_SHAPE, F32), HBM)],
    [HBM, VMEM],
    8,
    [pltpu.VMEM((N, EXPR_ROWS, LANES), F32), DMA((N,)), DMA((N,))],
    {0: 0},
)
order_dosage = call(
    dosage_kernel,
    "order_dosage",
    [(pltpu.HBM(DOSAGE_SHAPE, BF16), HBM)],
    [VMEM],
    16,
    [pltpu.VMEM(DOSAGE_SHAPE, BF16), DMA],
)
associate = call(
    association_kernel,
    "associate",
    [(jax.ShapeDtypeStruct((CT, OWN, WIN), F32), VMEM)],
    [VMEM, HBM, VMEM],
    16,
    [pltpu.VMEM(DOSAGE_SHAPE, BF16), pltpu.VMEM((N // 2, OWN * CT, LANES), F32), DMA],
)


def keep(array):
    return pltpu.with_memory_space_constraint(array, pltpu.HBM)


def per_device(counts, cell_donor, cell_type, covariates, dosage, windows):
    (parts,) = pack(
        keep(counts),
        keep(cell_donor.reshape(CHUNKS, LANES)),
        keep(cell_type.reshape(CHUNKS, LANES)),
        keep(covariates),
    )
    parts = lax.all_to_all(parts, "cell", 0, 0, tiled=True)
    (ordered,) = order_dosage(dosage)
    (library,) = sum_library(parts)
    library = lax.all_to_all(library, "gene", 0, 0, tiled=True)
    (sent,) = sum_cells(parts)
    (sent,) = express(keep(sent), library)
    sent = lax.all_to_all(sent, "donor", 0, 0, tiled=True)
    return associate(sent, keep(ordered), windows)[0]


def solution(mesh):
    in_specs = (
        P(("cell", "donor"), "gene"),
        P(("cell", "donor")),
        P(("cell", "donor")),
        P(("cell", "donor"), None),
        P("gene", None),
        P(("gene", "cell", "donor"), None),
    )
    out_specs = P(None, ("gene", "cell", "donor"), None)
    return jax.shard_map(
        per_device, mesh=mesh, in_specs=in_specs, out_specs=out_specs, check_vma=False
    )
```

```python
import math

import jax
import jax.numpy as jnp
from jax import lax
from jax.experimental import pallas as pl
from jax.experimental.pallas import tpu as pltpu
from jax.sharding import PartitionSpec as P

F32 = jnp.float32
BF16 = jnp.bfloat16
I32 = jnp.int32
HIGHEST = lax.Precision.HIGHEST

CT = 24
HALF = CT // 2
SUB = 8
NCOV = 50
ORDER = NCOV + 1
ORDER_ROWS = 56
N = 8
CELLS = 512
LANES = 128
CHUNKS = CELLS // LANES
GENES = 256
GENE_PART = GENES // N
OWN = GENE_PART // N
DON_GRP = 64
DONORS = N * DON_GRP
SNPS = 1024
WIN = 1024
SPAN = 256
PIECE = 64
DONOR_ROW = CHUNKS * GENE_PART
TYPE_ROW = DONOR_ROW + CHUNKS
TOTAL_ROW = TYPE_ROW + CHUNKS
COV_ROW = TOTAL_ROW + CHUNKS
PART_ROWS = COV_ROW + N // 2
SUM_ROWS = HALF * GENE_PART
LIB_ROWS = 16
EXPR_ROWS = HALF * OWN
SEND_ROWS = EXPR_ROWS + DON_GRP // 2

NT = (((1,), (1,)), ((), ()))
PLAIN = (((1,), (0,)), ((), ()))


def pack_kernel(
    counts_hbm, donor_hbm, type_hbm, cov_hbm, part_ref,
    counts_ref, donor_ref, type_ref, cov_ref, wide_ref, sems,
):
    copies = [
        pltpu.make_async_copy(
            counts_hbm.at[pl.ds(chunk * LANES, LANES)],
            counts_ref.at[pl.ds(chunk * LANES, LANES)],
            sems.at[chunk],
        )
        for chunk in range(CHUNKS)
    ]
    copies.append(pltpu.make_async_copy(donor_hbm, donor_ref, sems.at[CHUNKS]))
    copies.append(pltpu.make_async_copy(type_hbm, type_ref, sems.at[CHUNKS + 1]))
    copies.append(pltpu.make_async_copy(cov_hbm, cov_ref, sems.at[CHUNKS + 2]))
    for copy in copies:
        copy.start()
    totals = []
    for chunk in range(CHUNKS):
        copies[chunk].wait()
        turned = counts_ref[chunk * LANES : (chunk + 1) * LANES, :].astype(F32).T
        totals.append(jnp.sum(turned, axis=0, keepdims=True))
        for peer in range(N):
            part_ref[peer, chunk * GENE_PART : (chunk + 1) * GENE_PART, :] = turned[
                peer * GENE_PART : (peer + 1) * GENE_PART
            ]
    for copy in copies[CHUNKS:]:
        copy.wait()
    wide_ref[...] = jnp.zeros_like(wide_ref)
    wide_ref[:, :NCOV] = cov_ref[...]
    wide = wide_ref[...]
    paired = wide[: N // 2] + pltpu.roll(wide, DON_GRP, 1)[N // 2 :]
    shared = jnp.concatenate(
        [donor_ref[...].astype(F32), type_ref[...].astype(F32), *totals, paired], axis=0
    )
    for peer in range(N):
        part_ref[peer, DONOR_ROW:PART_ROWS, :] = shared


def to_row(block):
    return jnp.concatenate([block[row : row + 1] for row in range(CHUNKS)], axis=1)


def read_labels(part_ref, block):
    donor = part_ref[block, DONOR_ROW:TYPE_ROW, :].astype(I32)
    kind = part_ref[block, TYPE_ROW:TOTAL_ROW, :].astype(I32)
    local = ((donor >> 6) << 3) + (donor & 7)
    upper = kind >= HALF
    column = jnp.where(kind >= 0, jnp.where(upper, local + DON_GRP, local), -1)
    place = lax.broadcasted_iota(I32, (LANES, CELLS), 0)
    onehot = jnp.where(place == to_row(column), 1.0, 0.0).astype(BF16)
    return onehot, to_row(jnp.where(upper, kind - HALF, kind))


def library_kernel(part_ref, library_hbm, library_ref, sems):
    number = lax.broadcasted_iota(I32, (LIB_ROWS, CELLS), 0)
    summed = jnp.zeros((2 * LIB_ROWS, LANES), F32)
    for block in range(N):
        onehot, step = read_labels(part_ref, block)
        total = part_ref[block, TOTAL_ROW:COV_ROW, :]
        high = total.astype(BF16).astype(F32)
        left = jnp.concatenate(
            [jnp.where(number == step, to_row(value), 0.0) for value in (high, total - high)],
            axis=0,
        )
        summed = summed + lax.dot_general(
            left.astype(BF16), onehot, NT, preferred_element_type=F32
        )
    summed = summed[:LIB_ROWS] + summed[LIB_ROWS:]
    for group in range(HALF // OWN):
        library_ref[group] = summed[group * OWN : (group + 1) * OWN]
    copies = [
        pltpu.make_async_copy(library_ref, library_hbm.at[peer], sems.at[peer])
        for peer in range(N)
    ]
    for copy in copies:
        copy.start()
    for copy in copies:
        copy.wait()


def prepare_kernel(
    part_ref, dosage_ref, out_hbm, ordered_hbm, sum_ref, out_ref, ordered_ref, sems
):
    lane = lax.broadcasted_iota(I32, (SUB, LANES), 1)
    first_half = lax.broadcasted_iota(I32, (SUB, LANES), 0) < N // 2
    tiles = []
    for cell in range(N):
        tile = part_ref[cell, TOTAL_ROW:PART_ROWS, :]
        tile = jnp.where(first_half, pltpu.roll(tile, N // 2, 0), pltpu.roll(tile, DON_GRP, 1))
        tiles.append(jnp.where(lane < NCOV, tile, jnp.where(lane == NCOV, 1.0, 0.0)))
    tiles.append(jnp.zeros((DON_GRP, LANES), F32))
    turned = jnp.concatenate(tiles, axis=0).T
    design = turned[: DON_GRP // 2] + pltpu.roll(turned[DON_GRP // 2 : DON_GRP], DON_GRP, 1)
    for peer in range(N):
        out_ref[peer, EXPR_ROWS:, :] = design

    def one_block(block):
        onehot, step = read_labels(part_ref, block)
        counts = jnp.concatenate(
            [
                part_ref[block, chunk * GENE_PART : (chunk + 1) * GENE_PART, :]
                for chunk in range(CHUNKS)
            ],
            axis=1,
        )
        step = jnp.broadcast_to(step, (GENE_PART, CELLS))
        left = jnp.concatenate(
            [jnp.where(step == number, counts, 0.0).astype(BF16) for number in range(HALF)],
            axis=0,
        )
        return lax.dot_general(left, onehot, NT, preferred_element_type=F32)

    for block in range(0, N, 2):
        added = one_block(block) + one_block(block + 1)
        if block == 0:
            sum_ref[...] = added
        else:
            sum_ref[...] += added
    for step in range(HALF):
        logs = jnp.log2(sum_ref[step * GENE_PART : (step + 1) * GENE_PART, :] + 0.5)
        for peer in range(N):
            out_ref[peer, step * OWN : (step + 1) * OWN, :] = logs[peer * OWN : (peer + 1) * OWN]
    copies = [
        pltpu.make_async_copy(out_ref.at[peer], out_hbm.at[peer], sems.at[peer])
        for peer in range(N)
    ]
    for copy in copies:
        copy.start()
    place = lax.broadcasted_iota(I32, (DONORS, 1), 0)
    column = lax.broadcasted_iota(I32, (DONORS, DONORS), 1)
    source = (((place >> 3) & 7) << 6) + ((place >> 6) << 3) + (place & 7)
    order = jnp.where(column == source, 1.0, 0.0).astype(BF16)
    for index in range(SNPS // SPAN):
        span = pl.ds(index * SPAN, SPAN)
        half = dosage_ref[span, :].astype(F32).astype(BF16)
        moved = lax.dot_general(order, half, NT, preferred_element_type=F32)
        ordered_ref[:, span] = moved.astype(BF16)
        copies.append(
            pltpu.make_async_copy(
                ordered_ref.at[:, span], ordered_hbm.at[:, span], sems.at[N + index]
            )
        )
        copies[-1].start()
    for copy in copies:
        copy.wait()


def expression_kernel(sent_hbm, library_ref, out_ref, sems):
    arrivals = [
        pltpu.make_async_copy(sent_hbm.at[peer], out_ref.at[peer], sems.at[peer])
        for peer in range(N)
    ]
    for copy in arrivals:
        copy.start()
    library = library_ref[0]
    for peer in range(1, N):
        library = library + library_ref[peer]
    shift = math.log2(1000000.0) - jnp.log2(library + 1.0)
    shift = jnp.concatenate(
        [
            jnp.broadcast_to(shift[group, row : row + 1], (OWN, LANES))
            for group in range(HALF // OWN)
            for row in range(OWN)
        ],
        axis=0,
    )
    for peer in range(N):
        arrivals[peer].wait()
        out_ref[peer, :EXPR_ROWS, :] += shift


def association_kernel(
    recv_ref, dosage_hbm, windows_ref, out_ref, dosage_ref, expression_ref, sems
):
    copies = [
        pltpu.make_async_copy(
            dosage_hbm.at[pl.ds(start, PIECE)],
            dosage_ref.at[pl.ds(start, PIECE)],
            sems.at[start // PIECE],
        )
        for start in range(0, DONORS, PIECE)
    ]
    for copy in copies:
        copy.start()
    half_rows = DON_GRP // 2
    lane = lax.broadcasted_iota(I32, (half_rows, LANES), 1)
    lower, upper = [], []
    for pair in range(N // 2):
        one, two = recv_ref[2 * pair, EXPR_ROWS:, :], recv_ref[2 * pair + 1, EXPR_ROWS:, :]
        lower.append(jnp.where(lane < DON_GRP, one, pltpu.roll(two, DON_GRP, 1)))
        upper.append(jnp.where(lane < DON_GRP, pltpu.roll(one, DON_GRP, 1), two))
    turned = jnp.concatenate(
        [jnp.concatenate(lower, axis=1), jnp.concatenate(upper, axis=1)], axis=0
    )
    padded = jnp.concatenate([turned, jnp.zeros_like(turned)], axis=0)
    wide_lane = lax.broadcasted_iota(I32, (EXPR_ROWS, LANES), 1)
    for pair in range(N // 2):
        one, two = recv_ref[2 * pair, :EXPR_ROWS, :], recv_ref[2 * pair + 1, :EXPR_ROWS, :]
        expression_ref[pair, :EXPR_ROWS, :] = jnp.where(
            wide_lane < DON_GRP, one, pltpu.roll(two, DON_GRP, 1)
        )
        expression_ref[pair, EXPR_ROWS:, :] = jnp.where(
            wide_lane < DON_GRP, pltpu.roll(one, DON_GRP, 1), two
        )
    expression = jnp.concatenate(
        [
            jnp.concatenate(
                [
                    expression_ref[pair, pl.ds(gene, CT, stride=OWN), :]
                    for gene in range(OWN)
                ],
                axis=0,
            )
            for pair in range(N // 2)
        ],
        axis=1,
    )
    cross = lax.dot_general(expression, padded, NT, precision=HIGHEST, preferred_element_type=F32)
    gram = lax.dot_general(turned, padded, NT, precision=HIGHEST, preferred_element_type=F32)
    rows = ORDER_ROWS
    row_id = lax.broadcasted_iota(I32, (rows, LANES), 0)
    lane_id = lax.broadcasted_iota(I32, (rows, LANES), 1)
    row_col = lax.broadcasted_iota(I32, (rows, 1), 0)
    work = jnp.where(lane_id < 64, gram[:rows], jnp.where(lane_id - 64 == row_id, 1.0, 0.0))
    for panel in range(0, ORDER, SUB):
        members = range(panel, min(panel + SUB, ORDER))
        held = {
            column: jnp.broadcast_to(work[:, column : column + 1], (rows, LANES))
            for column in members
        }
        for column in members:
            mine = held[column]
            factor = jnp.where(row_id > column, mine, 0.0) * (1.0 / mine[column : column + 1])
            for later in range(column + 1, members.stop):
                held[later] = held[later] - factor * mine[later : later + 1]
            work = work - factor * work[column : column + 1]
    pivots = jnp.sum(jnp.where(lane_id == row_id, work, 0.0), axis=1, keepdims=True)
    scale = 1.0 / jnp.sqrt(jnp.where(row_col < ORDER, pivots, 1.0))
    inverse = pltpu.roll(work, 64, 1)
    inverse = jnp.where((lane_id < ORDER) & (row_id < ORDER), inverse * scale, 0.0)
    half_way = lax.dot_general(cross, inverse, NT, precision=HIGHEST, preferred_element_type=F32)
    coefficients = lax.dot_general(
        half_way, inverse, PLAIN, precision=HIGHEST, preferred_element_type=F32
    )
    residual = expression - lax.dot_general(
        coefficients, padded, PLAIN, precision=HIGHEST, preferred_element_type=F32
    )
    upper_part = residual.astype(BF16)
    lower_part = (residual - upper_part.astype(F32)).astype(BF16)
    for copy in copies:
        copy.wait()
    products = lax.dot_general(
        jnp.concatenate([upper_part, lower_part], axis=0),
        dosage_ref[...],
        PLAIN,
        preferred_element_type=F32,
    )
    both = OWN * CT
    products = (products[:both] + products[both:]) * (1.0 / math.sqrt(DONORS))
    windows = windows_ref[...]
    first_lane = lax.broadcasted_iota(I32, (1, LANES), 1) == 0
    for gene in range(OWN):
        first = jnp.where(first_lane, windows[gene : gene + 1, :LANES], 0).astype(F32)
        start = jnp.sum(first).astype(I32) & (SNPS - 1)
        turned_back = pltpu.roll(
            products[gene * CT : (gene + 1) * CT], (SNPS - start) & (SNPS - 1), 1
        )
        live = windows[gene : gene + 1] >= 0
        out_ref[:, gene, :] = jnp.where(live, turned_back, 0.0)


MIB = 1024 * 1024
HBM = pl.BlockSpec(memory_space=pltpu.HBM)


VMEM = pl.BlockSpec(memory_space=pltpu.VMEM)


def call(kernel, name, outs, ins, limit, scratch=(), aliases=None):
    return pl.pallas_call(
        kernel,
        name=name,
        out_shape=[out for out, _ in outs],
        in_specs=ins,
        out_specs=[spec for _, spec in outs],
        scratch_shapes=scratch,
        input_output_aliases=aliases or {},
        compiler_params=pltpu.CompilerParams(vmem_limit_bytes=limit * MIB),
    )


PART_SHAPE = (N, PART_ROWS, LANES)
SUM_SHAPE = (SUM_ROWS, LANES)
LIBRARY_SHAPE = (N, HALF // OWN, OWN, LANES)
SEND_SHAPE = (N, SEND_ROWS, LANES)
DOSAGE_SHAPE = (DONORS, SNPS)
DMA = pltpu.SemaphoreType.DMA

pack = call(
    pack_kernel,
    "pack",
    [(jax.ShapeDtypeStruct(PART_SHAPE, F32), VMEM)],
    [HBM] * 4,
    8,
    [
        pltpu.VMEM((CELLS, GENES), I32),
        pltpu.VMEM((CHUNKS, LANES), I32),
        pltpu.VMEM((CHUNKS, LANES), I32),
        pltpu.VMEM((N, NCOV), F32),
        pltpu.VMEM((N, LANES), F32),
        DMA((CHUNKS + 3,)),
    ],
)
sum_library = call(
    library_kernel,
    "sum_library",
    [(pltpu.HBM(LIBRARY_SHAPE, F32), HBM)],
    [VMEM],
    8,
    [pltpu.VMEM(LIBRARY_SHAPE[1:], F32), DMA((N,))],
)
prepare = call(
    prepare_kernel,
    "prepare",
    [(pltpu.HBM(SEND_SHAPE, F32), HBM), (pltpu.HBM(DOSAGE_SHAPE, BF16), HBM)],
    [VMEM, VMEM],
    16,
    [
        pltpu.VMEM(SUM_SHAPE, F32),
        pltpu.VMEM(SEND_SHAPE, F32),
        pltpu.VMEM(DOSAGE_SHAPE, BF16),
        DMA((N + SNPS // SPAN,)),
    ],
)
express = call(
    expression_kernel,
    "express",
    [(jax.ShapeDtypeStruct(SEND_SHAPE, F32), VMEM)],
    [HBM, VMEM],
    8,
    [DMA((N,))],
)
associate = call(
    association_kernel,
    "associate",
    [(jax.ShapeDtypeStruct((CT, OWN, WIN), F32), VMEM)],
    [VMEM, HBM, VMEM],
    16,
    [pltpu.VMEM(DOSAGE_SHAPE, BF16), pltpu.VMEM((N // 2, OWN * CT, LANES), F32), DMA((DONORS // PIECE,))],
)


def keep(array):
    return pltpu.with_memory_space_constraint(array, pltpu.HBM)


def per_device(counts, cell_donor, cell_type, covariates, dosage, windows):
    (parts,) = pack(
        keep(counts),
        keep(cell_donor.reshape(CHUNKS, LANES)),
        keep(cell_type.reshape(CHUNKS, LANES)),
        keep(covariates),
    )
    parts = lax.all_to_all(parts, "cell", 0, 0, tiled=True)
    (library,) = sum_library(parts)
    library = lax.all_to_all(library, "gene", 0, 0, tiled=True)
    sent, ordered = prepare(parts, dosage)
    (sent,) = express(keep(sent), library)
    sent = lax.all_to_all(sent, "donor", 0, 0, tiled=True)
    return associate(sent, keep(ordered), windows)[0]


def solution(mesh):
    in_specs = (
        P(("cell", "donor"), "gene"),
        P(("cell", "donor")),
        P(("cell", "donor")),
        P(("cell", "donor"), None),
        P("gene", None),
        P(("gene", "cell", "donor"), None),
    )
    out_specs = P(None, ("gene", "cell", "donor"), None)
    return jax.shard_map(
        per_device, mesh=mesh, in_specs=in_specs, out_specs=out_specs, check_vma=False
    )
```

```python
import math

import jax
import jax.numpy as jnp
from jax import lax
from jax.experimental import pallas as pl
from jax.experimental.pallas import tpu as pltpu
from jax.sharding import PartitionSpec as P

F32 = jnp.float32
BF16 = jnp.bfloat16
I32 = jnp.int32
HIGHEST = lax.Precision.HIGHEST

CT = 24
HALF = CT // 2
SUB = 8
NCOV = 50
ORDER = NCOV + 1
ORDER_ROWS = 56
N = 8
CELLS = 512
LANES = 128
CHUNKS = CELLS // LANES
GENES = 256
GENE_PART = GENES // N
OWN = GENE_PART // N
DON_GRP = 64
DONORS = N * DON_GRP
SNPS = 1024
WIN = 1024
SPAN = 256
PIECE = 64
PANEL = 17
DONOR_ROW = CHUNKS * GENE_PART
TYPE_ROW = DONOR_ROW + CHUNKS
TOTAL_ROW = TYPE_ROW + CHUNKS
COV_ROW = TOTAL_ROW + CHUNKS
PART_ROWS = COV_ROW + N // 2
SUM_ROWS = HALF * GENE_PART
LIB_ROWS = 16
EXPR_ROWS = HALF * OWN
SEND_ROWS = EXPR_ROWS + DON_GRP // 2

NT = (((1,), (1,)), ((), ()))
PLAIN = (((1,), (0,)), ((), ()))


def pack_kernel(
    counts_hbm, donor_hbm, type_hbm, cov_hbm, part_ref,
    counts_ref, donor_ref, type_ref, cov_ref, wide_ref, sems,
):
    copies = [
        pltpu.make_async_copy(
            counts_hbm.at[pl.ds(chunk * LANES, LANES)],
            counts_ref.at[pl.ds(chunk * LANES, LANES)],
            sems.at[chunk],
        )
        for chunk in range(CHUNKS)
    ]
    copies.append(pltpu.make_async_copy(donor_hbm, donor_ref, sems.at[CHUNKS]))
    copies.append(pltpu.make_async_copy(type_hbm, type_ref, sems.at[CHUNKS + 1]))
    copies.append(pltpu.make_async_copy(cov_hbm, cov_ref, sems.at[CHUNKS + 2]))
    for copy in copies:
        copy.start()
    totals = []
    for chunk in range(CHUNKS):
        copies[chunk].wait()
        turned = counts_ref[chunk * LANES : (chunk + 1) * LANES, :].astype(F32).T
        totals.append(jnp.sum(turned, axis=0, keepdims=True))
        for peer in range(N):
            part_ref[peer, chunk * GENE_PART : (chunk + 1) * GENE_PART, :] = turned[
                peer * GENE_PART : (peer + 1) * GENE_PART
            ]
    for copy in copies[CHUNKS:]:
        copy.wait()
    wide_ref[...] = jnp.zeros_like(wide_ref)
    wide_ref[:, :NCOV] = cov_ref[...]
    wide = wide_ref[...]
    paired = wide[: N // 2] + pltpu.roll(wide, DON_GRP, 1)[N // 2 :]
    shared = jnp.concatenate(
        [donor_ref[...].astype(F32), type_ref[...].astype(F32), *totals, paired], axis=0
    )
    for peer in range(N):
        part_ref[peer, DONOR_ROW:PART_ROWS, :] = shared


def to_row(block):
    return jnp.concatenate([block[row : row + 1] for row in range(CHUNKS)], axis=1)


def read_labels(part_ref, block):
    donor = part_ref[block, DONOR_ROW:TYPE_ROW, :].astype(I32)
    kind = part_ref[block, TYPE_ROW:TOTAL_ROW, :].astype(I32)
    local = ((donor >> 6) << 3) + (donor & 7)
    upper = kind >= HALF
    column = jnp.where(kind >= 0, jnp.where(upper, local + DON_GRP, local), -1)
    place = lax.broadcasted_iota(I32, (LANES, CELLS), 0)
    onehot = jnp.where(place == to_row(column), 1.0, 0.0).astype(BF16)
    return onehot, to_row(jnp.where(upper, kind - HALF, kind))


def library_kernel(part_ref, library_hbm, library_ref, sems):
    number = lax.broadcasted_iota(I32, (LIB_ROWS, CELLS), 0)
    summed = jnp.zeros((2 * LIB_ROWS, LANES), F32)
    for block in range(N):
        onehot, step = read_labels(part_ref, block)
        total = part_ref[block, TOTAL_ROW:COV_ROW, :]
        high = total.astype(BF16).astype(F32)
        left = jnp.concatenate(
            [jnp.where(number == step, to_row(value), 0.0) for value in (high, total - high)],
            axis=0,
        )
        summed = summed + lax.dot_general(
            left.astype(BF16), onehot, NT, preferred_element_type=F32
        )
    summed = summed[:LIB_ROWS] + summed[LIB_ROWS:]
    for group in range(HALF // OWN):
        library_ref[group] = summed[group * OWN : (group + 1) * OWN]
    copies = [
        pltpu.make_async_copy(library_ref, library_hbm.at[peer], sems.at[peer])
        for peer in range(N)
    ]
    for copy in copies:
        copy.start()
    for copy in copies:
        copy.wait()


def prepare_kernel(
    part_ref, dosage_ref, out_hbm, design_hbm, ordered_hbm,
    sum_ref, out_ref, design_ref, ordered_ref, sems,
):
    lane = lax.broadcasted_iota(I32, (SUB, LANES), 1)
    first_half = lax.broadcasted_iota(I32, (SUB, LANES), 0) < N // 2
    tiles = []
    for cell in range(N):
        tile = part_ref[cell, TOTAL_ROW:PART_ROWS, :]
        tile = jnp.where(first_half, pltpu.roll(tile, N // 2, 0), pltpu.roll(tile, DON_GRP, 1))
        tiles.append(jnp.where(lane < NCOV, tile, jnp.where(lane == NCOV, 1.0, 0.0)))
    tiles.append(jnp.zeros((DON_GRP, LANES), F32))
    turned = jnp.concatenate(tiles, axis=0).T
    design_ref[...] = turned[: DON_GRP // 2] + pltpu.roll(
        turned[DON_GRP // 2 : DON_GRP], DON_GRP, 1
    )

    def one_block(block):
        onehot, step = read_labels(part_ref, block)
        counts = jnp.concatenate(
            [
                part_ref[block, chunk * GENE_PART : (chunk + 1) * GENE_PART, :]
                for chunk in range(CHUNKS)
            ],
            axis=1,
        )
        step = jnp.broadcast_to(step, (GENE_PART, CELLS))
        left = jnp.concatenate(
            [jnp.where(step == number, counts, 0.0).astype(BF16) for number in range(HALF)],
            axis=0,
        )
        return lax.dot_general(left, onehot, NT, preferred_element_type=F32)

    for block in range(0, N, 2):
        added = one_block(block) + one_block(block + 1)
        if block == 0:
            sum_ref[...] = added
        else:
            sum_ref[...] += added
    for step in range(HALF):
        logs = jnp.log2(sum_ref[step * GENE_PART : (step + 1) * GENE_PART, :] + 0.5)
        for peer in range(N):
            out_ref[peer, step * OWN : (step + 1) * OWN, :] = logs[peer * OWN : (peer + 1) * OWN]
    copies = [
        pltpu.make_async_copy(out_ref.at[peer], out_hbm.at[peer], sems.at[peer])
        for peer in range(N)
    ]
    copies.append(pltpu.make_async_copy(design_ref, design_hbm, sems.at[N]))
    for copy in copies:
        copy.start()
    place = lax.broadcasted_iota(I32, (DONORS, 1), 0)
    column = lax.broadcasted_iota(I32, (DONORS, DONORS), 1)
    source = (((place >> 3) & 7) << 6) + ((place >> 6) << 3) + (place & 7)
    order = jnp.where(column == source, 1.0, 0.0).astype(BF16)
    for index in range(SNPS // SPAN):
        span = pl.ds(index * SPAN, SPAN)
        half = dosage_ref[span, :].astype(F32).astype(BF16)
        moved = lax.dot_general(order, half, NT, preferred_element_type=F32)
        ordered_ref[:, span] = moved.astype(BF16)
        copies.append(
            pltpu.make_async_copy(
                ordered_ref.at[:, span], ordered_hbm.at[:, span], sems.at[N + 1 + index]
            )
        )
        copies[-1].start()
    for copy in copies:
        copy.wait()


def expression_kernel(sent_hbm, design_hbm, library_ref, out_ref, design_ref, sems):
    arrivals = [
        pltpu.make_async_copy(
            sent_hbm.at[peer], out_ref.at[peer, pl.ds(0, EXPR_ROWS)], sems.at[peer]
        )
        for peer in range(N)
    ]
    arrivals.append(pltpu.make_async_copy(design_hbm, design_ref, sems.at[N]))
    for copy in arrivals:
        copy.start()
    library = library_ref[0]
    for peer in range(1, N):
        library = library + library_ref[peer]
    shift = math.log2(1000000.0) - jnp.log2(library + 1.0)
    shift = jnp.concatenate(
        [
            jnp.broadcast_to(shift[group, row : row + 1], (OWN, LANES))
            for group in range(HALF // OWN)
            for row in range(OWN)
        ],
        axis=0,
    )
    arrivals[N].wait()
    for peer in range(N):
        out_ref[peer, EXPR_ROWS:, :] = design_ref[...]
    for peer in range(N):
        arrivals[peer].wait()
        out_ref[peer, :EXPR_ROWS, :] += shift


def association_kernel(
    recv_ref, dosage_hbm, windows_ref, out_ref, dosage_ref, expression_ref, sems
):
    copies = [
        pltpu.make_async_copy(
            dosage_hbm.at[pl.ds(start, PIECE)],
            dosage_ref.at[pl.ds(start, PIECE)],
            sems.at[start // PIECE],
        )
        for start in range(0, DONORS, PIECE)
    ]
    for copy in copies:
        copy.start()
    half_rows = DON_GRP // 2
    lane = lax.broadcasted_iota(I32, (half_rows, LANES), 1)
    lower, upper = [], []
    for pair in range(N // 2):
        one, two = recv_ref[2 * pair, EXPR_ROWS:, :], recv_ref[2 * pair + 1, EXPR_ROWS:, :]
        lower.append(jnp.where(lane < DON_GRP, one, pltpu.roll(two, DON_GRP, 1)))
        upper.append(jnp.where(lane < DON_GRP, pltpu.roll(one, DON_GRP, 1), two))
    turned = jnp.concatenate(
        [jnp.concatenate(lower, axis=1), jnp.concatenate(upper, axis=1)], axis=0
    )
    padded = jnp.concatenate([turned, jnp.zeros_like(turned)], axis=0)
    wide_lane = lax.broadcasted_iota(I32, (EXPR_ROWS, LANES), 1)
    for pair in range(N // 2):
        one, two = recv_ref[2 * pair, :EXPR_ROWS, :], recv_ref[2 * pair + 1, :EXPR_ROWS, :]
        expression_ref[pair, :EXPR_ROWS, :] = jnp.where(
            wide_lane < DON_GRP, one, pltpu.roll(two, DON_GRP, 1)
        )
        expression_ref[pair, EXPR_ROWS:, :] = jnp.where(
            wide_lane < DON_GRP, pltpu.roll(one, DON_GRP, 1), two
        )
    expression = jnp.concatenate(
        [
            jnp.concatenate(
                [
                    expression_ref[pair, pl.ds(gene, CT, stride=OWN), :]
                    for gene in range(OWN)
                ],
                axis=0,
            )
            for pair in range(N // 2)
        ],
        axis=1,
    )
    cross = lax.dot_general(expression, padded, NT, precision=HIGHEST, preferred_element_type=F32)
    gram = lax.dot_general(turned, padded, NT, precision=HIGHEST, preferred_element_type=F32)
    rows = ORDER_ROWS
    row_id = lax.broadcasted_iota(I32, (rows, LANES), 0)
    lane_id = lax.broadcasted_iota(I32, (rows, LANES), 1)
    row_col = lax.broadcasted_iota(I32, (rows, 1), 0)
    work = jnp.where(lane_id < 64, gram[:rows], jnp.where(lane_id - 64 == row_id, 1.0, 0.0))
    for panel in range(0, ORDER, PANEL):
        members = range(panel, min(panel + PANEL, ORDER))
        base = panel // SUB * SUB
        live, live_id = work[base:], row_id[base:]
        held = {
            column: jnp.broadcast_to(live[:, column : column + 1], live.shape)
            for column in members
        }
        for column in members:
            mine = held[column]
            spot = column - base
            factor = jnp.where(live_id > column, mine, 0.0) * (1.0 / mine[spot : spot + 1])
            for later in range(column + 1, members.stop):
                held[later] = held[later] - factor * mine[later - base : later - base + 1]
            live = live - factor * live[spot : spot + 1]
        work = jnp.concatenate([work[:base], live], axis=0) if base else live
    pivots = jnp.sum(jnp.where(lane_id == row_id, work, 0.0), axis=1, keepdims=True)
    scale = 1.0 / jnp.sqrt(jnp.where(row_col < ORDER, pivots, 1.0))
    inverse = pltpu.roll(work, 64, 1)
    inverse = jnp.where((lane_id < ORDER) & (row_id < ORDER), inverse * scale, 0.0)
    half_way = lax.dot_general(cross, inverse, NT, precision=HIGHEST, preferred_element_type=F32)
    coefficients = lax.dot_general(
        half_way, inverse, PLAIN, precision=HIGHEST, preferred_element_type=F32
    )
    residual = expression - lax.dot_general(
        coefficients, padded, PLAIN, precision=HIGHEST, preferred_element_type=F32
    )
    upper_part = residual.astype(BF16)
    lower_part = (residual - upper_part.astype(F32)).astype(BF16)
    for copy in copies:
        copy.wait()
    products = lax.dot_general(
        jnp.concatenate([upper_part, lower_part], axis=0),
        dosage_ref[...],
        PLAIN,
        preferred_element_type=F32,
    )
    both = OWN * CT
    products = (products[:both] + products[both:]) * (1.0 / math.sqrt(DONORS))
    windows = windows_ref[...]
    first_lane = lax.broadcasted_iota(I32, (1, LANES), 1) == 0
    for gene in range(OWN):
        first = jnp.where(first_lane, windows[gene : gene + 1, :LANES], 0).astype(F32)
        start = jnp.sum(first).astype(I32) & (SNPS - 1)
        turned_back = pltpu.roll(
            products[gene * CT : (gene + 1) * CT], (SNPS - start) & (SNPS - 1), 1
        )
        live = windows[gene : gene + 1] >= 0
        out_ref[:, gene, :] = jnp.where(live, turned_back, 0.0)


MIB = 1024 * 1024
HBM = pl.BlockSpec(memory_space=pltpu.HBM)


VMEM = pl.BlockSpec(memory_space=pltpu.VMEM)


def call(kernel, name, outs, ins, limit, scratch=(), aliases=None):
    return pl.pallas_call(
        kernel,
        name=name,
        out_shape=[out for out, _ in outs],
        in_specs=ins,
        out_specs=[spec for _, spec in outs],
        scratch_shapes=scratch,
        input_output_aliases=aliases or {},
        compiler_params=pltpu.CompilerParams(vmem_limit_bytes=limit * MIB),
    )


PART_SHAPE = (N, PART_ROWS, LANES)
SUM_SHAPE = (SUM_ROWS, LANES)
LIBRARY_SHAPE = (N, HALF // OWN, OWN, LANES)
SEND_SHAPE = (N, SEND_ROWS, LANES)
LOG_SHAPE = (N, EXPR_ROWS, LANES)
DESIGN_SHAPE = (DON_GRP // 2, LANES)
DOSAGE_SHAPE = (DONORS, SNPS)
DMA = pltpu.SemaphoreType.DMA

pack = call(
    pack_kernel,
    "pack",
    [(jax.ShapeDtypeStruct(PART_SHAPE, F32), VMEM)],
    [HBM] * 4,
    8,
    [
        pltpu.VMEM((CELLS, GENES), I32),
        pltpu.VMEM((CHUNKS, LANES), I32),
        pltpu.VMEM((CHUNKS, LANES), I32),
        pltpu.VMEM((N, NCOV), F32),
        pltpu.VMEM((N, LANES), F32),
        DMA((CHUNKS + 3,)),
    ],
)
sum_library = call(
    library_kernel,
    "sum_library",
    [(pltpu.HBM(LIBRARY_SHAPE, F32), HBM)],
    [VMEM],
    8,
    [pltpu.VMEM(LIBRARY_SHAPE[1:], F32), DMA((N,))],
)
prepare = call(
    prepare_kernel,
    "prepare",
    [
        (pltpu.HBM(LOG_SHAPE, F32), HBM),
        (pltpu.HBM(DESIGN_SHAPE, F32), HBM),
        (pltpu.HBM(DOSAGE_SHAPE, BF16), HBM),
    ],
    [VMEM, VMEM],
    16,
    [
        pltpu.VMEM(SUM_SHAPE, F32),
        pltpu.VMEM(LOG_SHAPE, F32),
        pltpu.VMEM(DESIGN_SHAPE, F32),
        pltpu.VMEM(DOSAGE_SHAPE, BF16),
        DMA((N + 1 + SNPS // SPAN,)),
    ],
)
express = call(
    expression_kernel,
    "express",
    [(jax.ShapeDtypeStruct(SEND_SHAPE, F32), VMEM)],
    [HBM, HBM, VMEM],
    8,
    [pltpu.VMEM(DESIGN_SHAPE, F32), DMA((N + 1,))],
)
associate = call(
    association_kernel,
    "associate",
    [(jax.ShapeDtypeStruct((CT, OWN, WIN), F32), VMEM)],
    [VMEM, HBM, VMEM],
    16,
    [pltpu.VMEM(DOSAGE_SHAPE, BF16), pltpu.VMEM((N // 2, OWN * CT, LANES), F32), DMA((DONORS // PIECE,))],
)


def keep(array):
    return pltpu.with_memory_space_constraint(array, pltpu.HBM)


def per_device(counts, cell_donor, cell_type, covariates, dosage, windows):
    (parts,) = pack(
        keep(counts),
        keep(cell_donor.reshape(CHUNKS, LANES)),
        keep(cell_type.reshape(CHUNKS, LANES)),
        keep(covariates),
    )
    parts = lax.all_to_all(parts, "cell", 0, 0, tiled=True)
    (library,) = sum_library(parts)
    library = lax.all_to_all(library, "gene", 0, 0, tiled=True)
    logs, design, ordered = prepare(parts, dosage)
    (sent,) = express(keep(logs), keep(design), library)
    sent = lax.all_to_all(sent, "donor", 0, 0, tiled=True)
    return associate(sent, keep(ordered), windows)[0]


def solution(mesh):
    in_specs = (
        P(("cell", "donor"), "gene"),
        P(("cell", "donor")),
        P(("cell", "donor")),
        P(("cell", "donor"), None),
        P("gene", None),
        P(("gene", "cell", "donor"), None),
    )
    out_specs = P(None, ("gene", "cell", "donor"), None)
    return jax.shard_map(
        per_device, mesh=mesh, in_specs=in_specs, out_specs=out_specs, check_vma=False
    )
```

```python
import math

import jax
import jax.numpy as jnp
from jax import lax
from jax.experimental import pallas as pl
from jax.experimental.pallas import tpu as pltpu
from jax.sharding import PartitionSpec as P

F32 = jnp.float32
BF16 = jnp.bfloat16
I32 = jnp.int32
HIGHEST = lax.Precision.HIGHEST

CT = 24
HALF = CT // 2
SUB = 8
NCOV = 50
ORDER = NCOV + 1
ORDER_ROWS = 56
N = 8
CELLS = 512
LANES = 128
CHUNKS = CELLS // LANES
GENES = 256
GENE_PART = GENES // N
OWN = GENE_PART // N
DON_GRP = 64
DONORS = N * DON_GRP
SNPS = 1024
WIN = 1024
SPAN = 512
PIECE = 64
PANEL = 17
DONOR_ROW = CHUNKS * GENE_PART
TYPE_ROW = DONOR_ROW + CHUNKS
TOTAL_ROW = TYPE_ROW + CHUNKS
COV_ROW = TOTAL_ROW + CHUNKS
PART_ROWS = COV_ROW + N // 2
SUM_ROWS = HALF * GENE_PART
LIB_ROWS = 16
EXPR_ROWS = HALF * OWN
SEND_ROWS = EXPR_ROWS + DON_GRP // 2

NT = (((1,), (1,)), ((), ()))
PLAIN = (((1,), (0,)), ((), ()))


def pack_kernel(
    counts_hbm, donor_hbm, type_hbm, cov_hbm, part_ref,
    counts_ref, donor_ref, type_ref, cov_ref, wide_ref, sems,
):
    copies = [
        pltpu.make_async_copy(
            counts_hbm.at[pl.ds(chunk * LANES, LANES)],
            counts_ref.at[pl.ds(chunk * LANES, LANES)],
            sems.at[chunk],
        )
        for chunk in range(CHUNKS)
    ]
    copies.append(pltpu.make_async_copy(donor_hbm, donor_ref, sems.at[CHUNKS]))
    copies.append(pltpu.make_async_copy(type_hbm, type_ref, sems.at[CHUNKS + 1]))
    copies.append(pltpu.make_async_copy(cov_hbm, cov_ref, sems.at[CHUNKS + 2]))
    for copy in copies:
        copy.start()
    totals = []
    for chunk in range(CHUNKS):
        copies[chunk].wait()
        turned = counts_ref[chunk * LANES : (chunk + 1) * LANES, :].astype(F32).T
        totals.append(jnp.sum(turned, axis=0, keepdims=True))
        for peer in range(N):
            part_ref[peer, chunk * GENE_PART : (chunk + 1) * GENE_PART, :] = turned[
                peer * GENE_PART : (peer + 1) * GENE_PART
            ]
    for copy in copies[CHUNKS:]:
        copy.wait()
    wide_ref[...] = jnp.zeros_like(wide_ref)
    wide_ref[:, :NCOV] = cov_ref[...]
    wide = wide_ref[...]
    paired = wide[: N // 2] + pltpu.roll(wide, DON_GRP, 1)[N // 2 :]
    shared = jnp.concatenate(
        [donor_ref[...].astype(F32), type_ref[...].astype(F32), *totals, paired], axis=0
    )
    for peer in range(N):
        part_ref[peer, DONOR_ROW:PART_ROWS, :] = shared


def to_row(block):
    return jnp.concatenate([block[row : row + 1] for row in range(CHUNKS)], axis=1)


def read_labels(part_ref, block):
    donor = part_ref[block, DONOR_ROW:TYPE_ROW, :].astype(I32)
    kind = part_ref[block, TYPE_ROW:TOTAL_ROW, :].astype(I32)
    local = ((donor >> 6) << 3) + (donor & 7)
    upper = kind >= HALF
    column = jnp.where(kind >= 0, jnp.where(upper, local + DON_GRP, local), -1)
    place = lax.broadcasted_iota(I32, (LANES, CELLS), 0)
    onehot = jnp.where(place == to_row(column), 1.0, 0.0).astype(BF16)
    return onehot, to_row(jnp.where(upper, kind - HALF, kind))


def library_kernel(part_ref, library_hbm, library_ref, sems):
    number = lax.broadcasted_iota(I32, (LIB_ROWS, CELLS), 0)
    lefts, onehots = [], []
    for block in range(N):
        onehot, step = read_labels(part_ref, block)
        total = part_ref[block, TOTAL_ROW:COV_ROW, :]
        high = total.astype(BF16).astype(F32)
        left = jnp.concatenate(
            [jnp.where(number == step, to_row(value), 0.0) for value in (high, total - high)],
            axis=0,
        )
        lefts.append(left.astype(BF16))
        onehots.append(onehot)
    summed = lax.dot_general(
        jnp.concatenate(lefts, axis=1),
        jnp.concatenate(onehots, axis=1),
        NT,
        preferred_element_type=F32,
    )
    summed = summed[:LIB_ROWS] + summed[LIB_ROWS:]
    for group in range(HALF // OWN):
        library_ref[group] = summed[group * OWN : (group + 1) * OWN]
    copies = [
        pltpu.make_async_copy(library_ref, library_hbm.at[peer], sems.at[peer])
        for peer in range(N)
    ]
    for copy in copies:
        copy.start()
    for copy in copies:
        copy.wait()


def prepare_kernel(
    part_ref, dosage_ref, out_hbm, design_hbm, ordered_hbm,
    sum_ref, out_ref, design_ref, ordered_ref, sems,
):
    lane = lax.broadcasted_iota(I32, (SUB, LANES), 1)
    first_half = lax.broadcasted_iota(I32, (SUB, LANES), 0) < N // 2
    tiles = []
    for cell in range(N):
        tile = part_ref[cell, TOTAL_ROW:PART_ROWS, :]
        tile = jnp.where(first_half, pltpu.roll(tile, N // 2, 0), pltpu.roll(tile, DON_GRP, 1))
        tiles.append(jnp.where(lane < NCOV, tile, jnp.where(lane == NCOV, 1.0, 0.0)))
    tiles.append(jnp.zeros((DON_GRP, LANES), F32))
    turned = jnp.concatenate(tiles, axis=0).T
    design_ref[...] = turned[: DON_GRP // 2] + pltpu.roll(
        turned[DON_GRP // 2 : DON_GRP], DON_GRP, 1
    )

    def one_block(block):
        onehot, step = read_labels(part_ref, block)
        counts = jnp.concatenate(
            [
                part_ref[block, chunk * GENE_PART : (chunk + 1) * GENE_PART, :]
                for chunk in range(CHUNKS)
            ],
            axis=1,
        )
        step = jnp.broadcast_to(step, (GENE_PART, CELLS))
        left = jnp.concatenate(
            [jnp.where(step == number, counts, 0.0).astype(BF16) for number in range(HALF)],
            axis=0,
        )
        return lax.dot_general(left, onehot, NT, preferred_element_type=F32)

    for block in range(0, N, 2):
        added = one_block(block) + one_block(block + 1)
        if block == 0:
            sum_ref[...] = added
        else:
            sum_ref[...] += added
    for step in range(HALF):
        logs = jnp.log2(sum_ref[step * GENE_PART : (step + 1) * GENE_PART, :] + 0.5)
        for peer in range(N):
            out_ref[peer, step * OWN : (step + 1) * OWN, :] = logs[peer * OWN : (peer + 1) * OWN]
    copies = [
        pltpu.make_async_copy(out_ref.at[peer], out_hbm.at[peer], sems.at[peer])
        for peer in range(N)
    ]
    copies.append(pltpu.make_async_copy(design_ref, design_hbm, sems.at[N]))
    for copy in copies:
        copy.start()
    place = lax.broadcasted_iota(I32, (DONORS, 1), 0)
    column = lax.broadcasted_iota(I32, (DONORS, DONORS), 1)
    source = (((place >> 3) & 7) << 6) + ((place >> 6) << 3) + (place & 7)
    order = jnp.where(column == source, 1.0, 0.0).astype(BF16)
    for index in range(SNPS // SPAN):
        span = pl.ds(index * SPAN, SPAN)
        half = dosage_ref[span, :].astype(F32).astype(BF16)
        moved = lax.dot_general(order, half, NT, preferred_element_type=F32)
        ordered_ref[:, span] = moved.astype(BF16)
        copies.append(
            pltpu.make_async_copy(
                ordered_ref.at[:, span], ordered_hbm.at[:, span], sems.at[N + 1 + index]
            )
        )
        copies[-1].start()
    for copy in copies:
        copy.wait()


def expression_kernel(sent_hbm, design_hbm, library_ref, out_ref, design_ref, sems):
    arrivals = [
        pltpu.make_async_copy(
            sent_hbm.at[peer], out_ref.at[peer, pl.ds(0, EXPR_ROWS)], sems.at[peer]
        )
        for peer in range(N)
    ]
    arrivals.append(pltpu.make_async_copy(design_hbm, design_ref, sems.at[N]))
    for copy in arrivals:
        copy.start()
    library = library_ref[0]
    for peer in range(1, N):
        library = library + library_ref[peer]
    shift = math.log2(1000000.0) - jnp.log2(library + 1.0)
    shift = jnp.concatenate(
        [
            jnp.broadcast_to(shift[group, row : row + 1], (OWN, LANES))
            for group in range(HALF // OWN)
            for row in range(OWN)
        ],
        axis=0,
    )
    arrivals[N].wait()
    for peer in range(N):
        out_ref[peer, EXPR_ROWS:, :] = design_ref[...]
    for peer in range(N):
        arrivals[peer].wait()
        out_ref[peer, :EXPR_ROWS, :] += shift


def association_kernel(
    recv_ref, dosage_hbm, windows_ref, out_ref, dosage_ref, expression_ref, sems
):
    copies = [
        pltpu.make_async_copy(
            dosage_hbm.at[pl.ds(start, PIECE)],
            dosage_ref.at[pl.ds(start, PIECE)],
            sems.at[start // PIECE],
        )
        for start in range(0, DONORS, PIECE)
    ]
    for copy in copies:
        copy.start()
    half_rows = DON_GRP // 2
    lane = lax.broadcasted_iota(I32, (half_rows, LANES), 1)
    lower, upper = [], []
    for pair in range(N // 2):
        one, two = recv_ref[2 * pair, EXPR_ROWS:, :], recv_ref[2 * pair + 1, EXPR_ROWS:, :]
        lower.append(jnp.where(lane < DON_GRP, one, pltpu.roll(two, DON_GRP, 1)))
        upper.append(jnp.where(lane < DON_GRP, pltpu.roll(one, DON_GRP, 1), two))
    turned = jnp.concatenate(
        [jnp.concatenate(lower, axis=1), jnp.concatenate(upper, axis=1)], axis=0
    )
    padded = jnp.concatenate([turned, jnp.zeros_like(turned)], axis=0)
    wide_lane = lax.broadcasted_iota(I32, (EXPR_ROWS, LANES), 1)
    for pair in range(N // 2):
        one, two = recv_ref[2 * pair, :EXPR_ROWS, :], recv_ref[2 * pair + 1, :EXPR_ROWS, :]
        expression_ref[pair, :EXPR_ROWS, :] = jnp.where(
            wide_lane < DON_GRP, one, pltpu.roll(two, DON_GRP, 1)
        )
        expression_ref[pair, EXPR_ROWS:, :] = jnp.where(
            wide_lane < DON_GRP, pltpu.roll(one, DON_GRP, 1), two
        )
    expression = jnp.concatenate(
        [
            jnp.concatenate(
                [
                    expression_ref[pair, pl.ds(gene, CT, stride=OWN), :]
                    for gene in range(OWN)
                ],
                axis=0,
            )
            for pair in range(N // 2)
        ],
        axis=1,
    )
    cross = lax.dot_general(expression, padded, NT, precision=HIGHEST, preferred_element_type=F32)
    gram = lax.dot_general(turned, padded, NT, precision=HIGHEST, preferred_element_type=F32)
    rows = ORDER_ROWS
    row_id = lax.broadcasted_iota(I32, (rows, LANES), 0)
    lane_id = lax.broadcasted_iota(I32, (rows, LANES), 1)
    row_col = lax.broadcasted_iota(I32, (rows, 1), 0)
    work = jnp.where(lane_id < 64, gram[:rows], jnp.where(lane_id - 64 == row_id, 1.0, 0.0))
    for panel in range(0, ORDER, PANEL):
        members = range(panel, min(panel + PANEL, ORDER))
        base = panel // SUB * SUB
        live, live_id = work[base:], row_id[base:]
        held = {
            column: jnp.broadcast_to(live[:, column : column + 1], live.shape)
            for column in members
        }
        for column in members:
            mine = held[column]
            spot = column - base
            factor = jnp.where(live_id > column, mine, 0.0) * (1.0 / mine[spot : spot + 1])
            for later in range(column + 1, members.stop):
                held[later] = held[later] - factor * mine[later - base : later - base + 1]
            live = live - factor * live[spot : spot + 1]
        work = jnp.concatenate([work[:base], live], axis=0) if base else live
    pivots = jnp.sum(jnp.where(lane_id == row_id, work, 0.0), axis=1, keepdims=True)
    scale = 1.0 / jnp.sqrt(jnp.where(row_col < ORDER, pivots, 1.0))
    inverse = pltpu.roll(work, 64, 1)
    inverse = jnp.where((lane_id < ORDER) & (row_id < ORDER), inverse * scale, 0.0)
    half_way = lax.dot_general(cross, inverse, NT, precision=HIGHEST, preferred_element_type=F32)
    coefficients = lax.dot_general(
        half_way, inverse, PLAIN, precision=HIGHEST, preferred_element_type=F32
    )
    residual = expression - lax.dot_general(
        coefficients, padded, PLAIN, precision=HIGHEST, preferred_element_type=F32
    )
    upper_part = residual.astype(BF16)
    lower_part = (residual - upper_part.astype(F32)).astype(BF16)
    for copy in copies:
        copy.wait()
    products = lax.dot_general(
        jnp.concatenate([upper_part, lower_part], axis=0),
        dosage_ref[...],
        PLAIN,
        preferred_element_type=F32,
    )
    both = OWN * CT
    products = (products[:both] + products[both:]) * (1.0 / math.sqrt(DONORS))
    windows = windows_ref[...]
    first_lane = lax.broadcasted_iota(I32, (1, LANES), 1) == 0
    for gene in range(OWN):
        first = jnp.where(first_lane, windows[gene : gene + 1, :LANES], 0).astype(F32)
        start = jnp.sum(first).astype(I32) & (SNPS - 1)
        turned_back = pltpu.roll(
            products[gene * CT : (gene + 1) * CT], (SNPS - start) & (SNPS - 1), 1
        )
        live = windows[gene : gene + 1] >= 0
        out_ref[:, gene, :] = jnp.where(live, turned_back, 0.0)


MIB = 1024 * 1024
HBM = pl.BlockSpec(memory_space=pltpu.HBM)


VMEM = pl.BlockSpec(memory_space=pltpu.VMEM)


def call(kernel, name, outs, ins, limit, scratch=(), aliases=None):
    return pl.pallas_call(
        kernel,
        name=name,
        out_shape=[out for out, _ in outs],
        in_specs=ins,
        out_specs=[spec for _, spec in outs],
        scratch_shapes=scratch,
        input_output_aliases=aliases or {},
        compiler_params=pltpu.CompilerParams(vmem_limit_bytes=limit * MIB),
    )


PART_SHAPE = (N, PART_ROWS, LANES)
SUM_SHAPE = (SUM_ROWS, LANES)
LIBRARY_SHAPE = (N, HALF // OWN, OWN, LANES)
SEND_SHAPE = (N, SEND_ROWS, LANES)
LOG_SHAPE = (N, EXPR_ROWS, LANES)
DESIGN_SHAPE = (DON_GRP // 2, LANES)
DOSAGE_SHAPE = (DONORS, SNPS)
DMA = pltpu.SemaphoreType.DMA

pack = call(
    pack_kernel,
    "pack",
    [(jax.ShapeDtypeStruct(PART_SHAPE, F32), VMEM)],
    [HBM] * 4,
    8,
    [
        pltpu.VMEM((CELLS, GENES), I32),
        pltpu.VMEM((CHUNKS, LANES), I32),
        pltpu.VMEM((CHUNKS, LANES), I32),
        pltpu.VMEM((N, NCOV), F32),
        pltpu.VMEM((N, LANES), F32),
        DMA((CHUNKS + 3,)),
    ],
)
sum_library = call(
    library_kernel,
    "sum_library",
    [(pltpu.HBM(LIBRARY_SHAPE, F32), HBM)],
    [VMEM],
    8,
    [pltpu.VMEM(LIBRARY_SHAPE[1:], F32), DMA((N,))],
)
prepare = call(
    prepare_kernel,
    "prepare",
    [
        (pltpu.HBM(LOG_SHAPE, F32), HBM),
        (pltpu.HBM(DESIGN_SHAPE, F32), HBM),
        (pltpu.HBM(DOSAGE_SHAPE, BF16), HBM),
    ],
    [VMEM, VMEM],
    16,
    [
        pltpu.VMEM(SUM_SHAPE, F32),
        pltpu.VMEM(LOG_SHAPE, F32),
        pltpu.VMEM(DESIGN_SHAPE, F32),
        pltpu.VMEM(DOSAGE_SHAPE, BF16),
        DMA((N + 1 + SNPS // SPAN,)),
    ],
)
express = call(
    expression_kernel,
    "express",
    [(jax.ShapeDtypeStruct(SEND_SHAPE, F32), VMEM)],
    [HBM, HBM, VMEM],
    8,
    [pltpu.VMEM(DESIGN_SHAPE, F32), DMA((N + 1,))],
)
associate = call(
    association_kernel,
    "associate",
    [(jax.ShapeDtypeStruct((CT, OWN, WIN), F32), VMEM)],
    [VMEM, HBM, VMEM],
    16,
    [pltpu.VMEM(DOSAGE_SHAPE, BF16), pltpu.VMEM((N // 2, OWN * CT, LANES), F32), DMA((DONORS // PIECE,))],
)


def keep(array):
    return pltpu.with_memory_space_constraint(array, pltpu.HBM)


def per_device(counts, cell_donor, cell_type, covariates, dosage, windows):
    (parts,) = pack(
        keep(counts),
        keep(cell_donor.reshape(CHUNKS, LANES)),
        keep(cell_type.reshape(CHUNKS, LANES)),
        keep(covariates),
    )
    parts = lax.all_to_all(parts, "cell", 0, 0, tiled=True)
    (library,) = sum_library(parts)
    library = lax.all_to_all(library, "gene", 0, 0, tiled=True)
    logs, design, ordered = prepare(parts, dosage)
    (sent,) = express(keep(logs), keep(design), library)
    sent = lax.all_to_all(sent, "donor", 0, 0, tiled=True)
    return associate(sent, keep(ordered), windows)[0]


def solution(mesh):
    in_specs = (
        P(("cell", "donor"), "gene"),
        P(("cell", "donor")),
        P(("cell", "donor")),
        P(("cell", "donor"), None),
        P("gene", None),
        P(("gene", "cell", "donor"), None),
    )
    out_specs = P(None, ("gene", "cell", "donor"), None)
    return jax.shard_map(
        per_device, mesh=mesh, in_specs=in_specs, out_specs=out_specs, check_vma=False
    )
```

```python
import math

import jax
import jax.numpy as jnp
from jax import lax
from jax.experimental import pallas as pl
from jax.experimental.pallas import tpu as pltpu
from jax.sharding import PartitionSpec as P

F32 = jnp.float32
BF16 = jnp.bfloat16
I32 = jnp.int32
HIGHEST = lax.Precision.HIGHEST

CT = 24
HALF = CT // 2
SUB = 8
NCOV = 50
ORDER = NCOV + 1
ORDER_ROWS = 56
N = 8
CELLS = 512
LANES = 128
CHUNKS = CELLS // LANES
GENES = 256
GENE_PART = GENES // N
OWN = GENE_PART // N
DON_GRP = 64
DONORS = N * DON_GRP
SNPS = 1024
WIN = 1024
SPANS = ((0, 512), (512, 256), (768, 256))
PIECE = 64
PANEL = 17
DONOR_ROW = CHUNKS * GENE_PART
TYPE_ROW = DONOR_ROW + CHUNKS
TOTAL_ROW = TYPE_ROW + CHUNKS
COV_ROW = TOTAL_ROW + CHUNKS
PART_ROWS = COV_ROW + N // 2
SUM_ROWS = HALF * GENE_PART
LIB_ROWS = 16
EXPR_ROWS = HALF * OWN
SEND_ROWS = EXPR_ROWS + DON_GRP // 2

NT = (((1,), (1,)), ((), ()))
PLAIN = (((1,), (0,)), ((), ()))


def pack_kernel(
    counts_hbm, donor_hbm, type_hbm, cov_hbm, part_ref,
    counts_ref, donor_ref, type_ref, cov_ref, wide_ref, sems,
):
    copies = [
        pltpu.make_async_copy(
            counts_hbm.at[pl.ds(chunk * LANES, LANES)],
            counts_ref.at[pl.ds(chunk * LANES, LANES)],
            sems.at[chunk],
        )
        for chunk in range(CHUNKS)
    ]
    copies.append(pltpu.make_async_copy(donor_hbm, donor_ref, sems.at[CHUNKS]))
    copies.append(pltpu.make_async_copy(type_hbm, type_ref, sems.at[CHUNKS + 1]))
    copies.append(pltpu.make_async_copy(cov_hbm, cov_ref, sems.at[CHUNKS + 2]))
    for copy in copies:
        copy.start()
    totals = []
    for chunk in range(CHUNKS):
        copies[chunk].wait()
        turned = counts_ref[chunk * LANES : (chunk + 1) * LANES, :].astype(F32).T
        totals.append(jnp.sum(turned, axis=0, keepdims=True))
        for peer in range(N):
            part_ref[peer, chunk * GENE_PART : (chunk + 1) * GENE_PART, :] = turned[
                peer * GENE_PART : (peer + 1) * GENE_PART
            ]
    for copy in copies[CHUNKS:]:
        copy.wait()
    wide_ref[...] = jnp.zeros_like(wide_ref)
    wide_ref[:, :NCOV] = cov_ref[...]
    wide = wide_ref[...]
    paired = wide[: N // 2] + pltpu.roll(wide, DON_GRP, 1)[N // 2 :]
    shared = jnp.concatenate(
        [donor_ref[...].astype(F32), type_ref[...].astype(F32), *totals, paired], axis=0
    )
    for peer in range(N):
        part_ref[peer, DONOR_ROW:PART_ROWS, :] = shared


def to_row(block):
    return jnp.concatenate([block[row : row + 1] for row in range(CHUNKS)], axis=1)


def read_labels(part_ref, block):
    donor = part_ref[block, DONOR_ROW:TYPE_ROW, :].astype(I32)
    kind = part_ref[block, TYPE_ROW:TOTAL_ROW, :].astype(I32)
    local = ((donor >> 6) << 3) + (donor & 7)
    upper = kind >= HALF
    column = jnp.where(kind >= 0, jnp.where(upper, local + DON_GRP, local), -1)
    place = lax.broadcasted_iota(I32, (LANES, CELLS), 0)
    onehot = jnp.where(place == to_row(column), 1.0, 0.0).astype(BF16)
    return onehot, to_row(jnp.where(upper, kind - HALF, kind))


def library_kernel(part_ref, library_hbm, library_ref, sems):
    number = lax.broadcasted_iota(I32, (LIB_ROWS, CELLS), 0)
    lefts, onehots = [], []
    for block in range(N):
        onehot, step = read_labels(part_ref, block)
        total = part_ref[block, TOTAL_ROW:COV_ROW, :]
        high = total.astype(BF16).astype(F32)
        left = jnp.concatenate(
            [jnp.where(number == step, to_row(value), 0.0) for value in (high, total - high)],
            axis=0,
        )
        lefts.append(left.astype(BF16))
        onehots.append(onehot)
    summed = lax.dot_general(
        jnp.concatenate(lefts, axis=1),
        jnp.concatenate(onehots, axis=1),
        NT,
        preferred_element_type=F32,
    )
    summed = summed[:LIB_ROWS] + summed[LIB_ROWS:]
    for group in range(HALF // OWN):
        library_ref[group] = summed[group * OWN : (group + 1) * OWN]
    copies = [
        pltpu.make_async_copy(library_ref, library_hbm.at[peer], sems.at[peer])
        for peer in range(N)
    ]
    for copy in copies:
        copy.start()
    for copy in copies:
        copy.wait()


def prepare_kernel(
    part_ref, dosage_ref, out_hbm, design_hbm, ordered_hbm,
    sum_ref, out_ref, design_ref, ordered_ref, sems,
):
    lane = lax.broadcasted_iota(I32, (SUB, LANES), 1)
    first_half = lax.broadcasted_iota(I32, (SUB, LANES), 0) < N // 2
    tiles = []
    for cell in range(N):
        tile = part_ref[cell, TOTAL_ROW:PART_ROWS, :]
        tile = jnp.where(first_half, pltpu.roll(tile, N // 2, 0), pltpu.roll(tile, DON_GRP, 1))
        tiles.append(jnp.where(lane < NCOV, tile, jnp.where(lane == NCOV, 1.0, 0.0)))
    tiles.append(jnp.zeros((DON_GRP, LANES), F32))
    turned = jnp.concatenate(tiles, axis=0).T
    design_ref[...] = turned[: DON_GRP // 2] + pltpu.roll(
        turned[DON_GRP // 2 : DON_GRP], DON_GRP, 1
    )

    def one_block(block):
        onehot, step = read_labels(part_ref, block)
        counts = jnp.concatenate(
            [
                part_ref[block, chunk * GENE_PART : (chunk + 1) * GENE_PART, :]
                for chunk in range(CHUNKS)
            ],
            axis=1,
        )
        step = jnp.broadcast_to(step, (GENE_PART, CELLS))
        left = jnp.concatenate(
            [jnp.where(step == number, counts, 0.0).astype(BF16) for number in range(HALF)],
            axis=0,
        )
        return lax.dot_general(left, onehot, NT, preferred_element_type=F32)

    for block in range(0, N, 2):
        added = one_block(block) + one_block(block + 1)
        if block == 0:
            sum_ref[...] = added
        else:
            sum_ref[...] += added
    for step in range(HALF):
        logs = jnp.log2(sum_ref[step * GENE_PART : (step + 1) * GENE_PART, :] + 0.5)
        for peer in range(N):
            out_ref[peer, step * OWN : (step + 1) * OWN, :] = logs[peer * OWN : (peer + 1) * OWN]
    copies = [
        pltpu.make_async_copy(out_ref.at[peer], out_hbm.at[peer], sems.at[peer])
        for peer in range(N)
    ]
    copies.append(pltpu.make_async_copy(design_ref, design_hbm, sems.at[N]))
    for copy in copies:
        copy.start()
    place = lax.broadcasted_iota(I32, (DONORS, 1), 0)
    column = lax.broadcasted_iota(I32, (DONORS, DONORS), 1)
    source = (((place >> 3) & 7) << 6) + ((place >> 6) << 3) + (place & 7)
    order = jnp.where(column == source, 1.0, 0.0).astype(BF16)
    for index, (begin, size) in enumerate(SPANS):
        span = pl.ds(begin, size)
        half = dosage_ref[span, :].astype(F32).astype(BF16)
        moved = lax.dot_general(order, half, NT, preferred_element_type=F32)
        ordered_ref[:, span] = moved.astype(BF16)
        copies.append(
            pltpu.make_async_copy(
                ordered_ref.at[:, span], ordered_hbm.at[:, span], sems.at[N + 1 + index]
            )
        )
        copies[-1].start()
    for copy in copies:
        copy.wait()


def expression_kernel(sent_hbm, design_hbm, library_ref, out_ref, design_ref, sems):
    arrivals = [
        pltpu.make_async_copy(
            sent_hbm.at[peer], out_ref.at[peer, pl.ds(0, EXPR_ROWS)], sems.at[peer]
        )
        for peer in range(N)
    ]
    arrivals.append(pltpu.make_async_copy(design_hbm, design_ref, sems.at[N]))
    for copy in arrivals:
        copy.start()
    library = library_ref[0]
    for peer in range(1, N):
        library = library + library_ref[peer]
    shift = math.log2(1000000.0) - jnp.log2(library + 1.0)
    shift = jnp.concatenate(
        [
            jnp.broadcast_to(shift[group, row : row + 1], (OWN, LANES))
            for group in range(HALF // OWN)
            for row in range(OWN)
        ],
        axis=0,
    )
    arrivals[N].wait()
    for peer in range(N):
        out_ref[peer, EXPR_ROWS:, :] = design_ref[...]
    for peer in range(N):
        arrivals[peer].wait()
        out_ref[peer, :EXPR_ROWS, :] += shift


def association_kernel(
    recv_ref, dosage_hbm, windows_ref, out_ref, dosage_ref, expression_ref, sems
):
    copies = [
        pltpu.make_async_copy(
            dosage_hbm.at[pl.ds(start, PIECE)],
            dosage_ref.at[pl.ds(start, PIECE)],
            sems.at[start // PIECE],
        )
        for start in range(0, DONORS, PIECE)
    ]
    for copy in copies:
        copy.start()
    half_rows = DON_GRP // 2
    lane = lax.broadcasted_iota(I32, (half_rows, LANES), 1)
    lower, upper = [], []
    for pair in range(N // 2):
        one, two = recv_ref[2 * pair, EXPR_ROWS:, :], recv_ref[2 * pair + 1, EXPR_ROWS:, :]
        lower.append(jnp.where(lane < DON_GRP, one, pltpu.roll(two, DON_GRP, 1)))
        upper.append(jnp.where(lane < DON_GRP, pltpu.roll(one, DON_GRP, 1), two))
    turned = jnp.concatenate(
        [jnp.concatenate(lower, axis=1), jnp.concatenate(upper, axis=1)], axis=0
    )
    padded = jnp.concatenate([turned, jnp.zeros_like(turned)], axis=0)
    wide_lane = lax.broadcasted_iota(I32, (EXPR_ROWS, LANES), 1)
    for pair in range(N // 2):
        one, two = recv_ref[2 * pair, :EXPR_ROWS, :], recv_ref[2 * pair + 1, :EXPR_ROWS, :]
        expression_ref[pair, :EXPR_ROWS, :] = jnp.where(
            wide_lane < DON_GRP, one, pltpu.roll(two, DON_GRP, 1)
        )
        expression_ref[pair, EXPR_ROWS:, :] = jnp.where(
            wide_lane < DON_GRP, pltpu.roll(one, DON_GRP, 1), two
        )
    expression = jnp.concatenate(
        [
            jnp.concatenate(
                [
                    expression_ref[pair, pl.ds(gene, CT, stride=OWN), :]
                    for gene in range(OWN)
                ],
                axis=0,
            )
            for pair in range(N // 2)
        ],
        axis=1,
    )
    cross = lax.dot_general(expression, padded, NT, precision=HIGHEST, preferred_element_type=F32)
    gram = lax.dot_general(turned, padded, NT, precision=HIGHEST, preferred_element_type=F32)
    rows = ORDER_ROWS
    row_id = lax.broadcasted_iota(I32, (rows, LANES), 0)
    lane_id = lax.broadcasted_iota(I32, (rows, LANES), 1)
    row_col = lax.broadcasted_iota(I32, (rows, 1), 0)
    work = jnp.where(lane_id < 64, gram[:rows], jnp.where(lane_id - 64 == row_id, 1.0, 0.0))
    for panel in range(0, ORDER, PANEL):
        members = range(panel, min(panel + PANEL, ORDER))
        base = panel // SUB * SUB
        live, live_id = work[base:], row_id[base:]
        held = {
            column: jnp.broadcast_to(live[:, column : column + 1], live.shape)
            for column in members
        }
        for column in members:
            mine = held[column]
            spot = column - base
            factor = jnp.where(live_id > column, mine, 0.0) * (1.0 / mine[spot : spot + 1])
            for later in range(column + 1, members.stop):
                held[later] = held[later] - factor * mine[later - base : later - base + 1]
            live = live - factor * live[spot : spot + 1]
        work = jnp.concatenate([work[:base], live], axis=0) if base else live
    pivots = jnp.sum(jnp.where(lane_id == row_id, work, 0.0), axis=1, keepdims=True)
    scale = 1.0 / jnp.sqrt(jnp.where(row_col < ORDER, pivots, 1.0))
    inverse = pltpu.roll(work, 64, 1)
    inverse = jnp.where((lane_id < ORDER) & (row_id < ORDER), inverse * scale, 0.0)
    half_way = lax.dot_general(cross, inverse, NT, precision=HIGHEST, preferred_element_type=F32)
    coefficients = lax.dot_general(
        half_way, inverse, PLAIN, precision=HIGHEST, preferred_element_type=F32
    )
    residual = expression - lax.dot_general(
        coefficients, padded, PLAIN, precision=HIGHEST, preferred_element_type=F32
    )
    upper_part = residual.astype(BF16)
    lower_part = (residual - upper_part.astype(F32)).astype(BF16)
    for copy in copies:
        copy.wait()
    products = lax.dot_general(
        jnp.concatenate([upper_part, lower_part], axis=0),
        dosage_ref[...],
        PLAIN,
        preferred_element_type=F32,
    )
    both = OWN * CT
    products = (products[:both] + products[both:]) * (1.0 / math.sqrt(DONORS))
    windows = windows_ref[...]
    first_lane = lax.broadcasted_iota(I32, (1, LANES), 1) == 0
    for gene in range(OWN):
        first = jnp.where(first_lane, windows[gene : gene + 1, :LANES], 0).astype(F32)
        start = jnp.sum(first).astype(I32) & (SNPS - 1)
        turned_back = pltpu.roll(
            products[gene * CT : (gene + 1) * CT], (SNPS - start) & (SNPS - 1), 1
        )
        live = windows[gene : gene + 1] >= 0
        out_ref[:, gene, :] = jnp.where(live, turned_back, 0.0)


MIB = 1024 * 1024
HBM = pl.BlockSpec(memory_space=pltpu.HBM)


VMEM = pl.BlockSpec(memory_space=pltpu.VMEM)


def call(kernel, name, outs, ins, limit, scratch=(), aliases=None):
    return pl.pallas_call(
        kernel,
        name=name,
        out_shape=[out for out, _ in outs],
        in_specs=ins,
        out_specs=[spec for _, spec in outs],
        scratch_shapes=scratch,
        input_output_aliases=aliases or {},
        compiler_params=pltpu.CompilerParams(vmem_limit_bytes=limit * MIB),
    )


PART_SHAPE = (N, PART_ROWS, LANES)
SUM_SHAPE = (SUM_ROWS, LANES)
LIBRARY_SHAPE = (N, HALF // OWN, OWN, LANES)
SEND_SHAPE = (N, SEND_ROWS, LANES)
LOG_SHAPE = (N, EXPR_ROWS, LANES)
DESIGN_SHAPE = (DON_GRP // 2, LANES)
DOSAGE_SHAPE = (DONORS, SNPS)
DMA = pltpu.SemaphoreType.DMA

pack = call(
    pack_kernel,
    "pack",
    [(jax.ShapeDtypeStruct(PART_SHAPE, F32), VMEM)],
    [HBM] * 4,
    8,
    [
        pltpu.VMEM((CELLS, GENES), I32),
        pltpu.VMEM((CHUNKS, LANES), I32),
        pltpu.VMEM((CHUNKS, LANES), I32),
        pltpu.VMEM((N, NCOV), F32),
        pltpu.VMEM((N, LANES), F32),
        DMA((CHUNKS + 3,)),
    ],
)
sum_library = call(
    library_kernel,
    "sum_library",
    [(pltpu.HBM(LIBRARY_SHAPE, F32), HBM)],
    [VMEM],
    8,
    [pltpu.VMEM(LIBRARY_SHAPE[1:], F32), DMA((N,))],
)
prepare = call(
    prepare_kernel,
    "prepare",
    [
        (pltpu.HBM(LOG_SHAPE, F32), HBM),
        (pltpu.HBM(DESIGN_SHAPE, F32), HBM),
        (pltpu.HBM(DOSAGE_SHAPE, BF16), HBM),
    ],
    [VMEM, VMEM],
    16,
    [
        pltpu.VMEM(SUM_SHAPE, F32),
        pltpu.VMEM(LOG_SHAPE, F32),
        pltpu.VMEM(DESIGN_SHAPE, F32),
        pltpu.VMEM(DOSAGE_SHAPE, BF16),
        DMA((N + 1 + len(SPANS),)),
    ],
)
express = call(
    expression_kernel,
    "express",
    [(jax.ShapeDtypeStruct(SEND_SHAPE, F32), VMEM)],
    [HBM, HBM, VMEM],
    8,
    [pltpu.VMEM(DESIGN_SHAPE, F32), DMA((N + 1,))],
)
associate = call(
    association_kernel,
    "associate",
    [(jax.ShapeDtypeStruct((CT, OWN, WIN), F32), VMEM)],
    [VMEM, HBM, VMEM],
    16,
    [pltpu.VMEM(DOSAGE_SHAPE, BF16), pltpu.VMEM((N // 2, OWN * CT, LANES), F32), DMA((DONORS // PIECE,))],
)


def keep(array):
    return pltpu.with_memory_space_constraint(array, pltpu.HBM)


def per_device(counts, cell_donor, cell_type, covariates, dosage, windows):
    (parts,) = pack(
        keep(counts),
        keep(cell_donor.reshape(CHUNKS, LANES)),
        keep(cell_type.reshape(CHUNKS, LANES)),
        keep(covariates),
    )
    parts = lax.all_to_all(parts, "cell", 0, 0, tiled=True)
    (library,) = sum_library(parts)
    library = lax.all_to_all(library, "gene", 0, 0, tiled=True)
    logs, design, ordered = prepare(parts, dosage)
    (sent,) = express(keep(logs), keep(design), library)
    sent = lax.all_to_all(sent, "donor", 0, 0, tiled=True)
    return associate(sent, keep(ordered), windows)[0]


def solution(mesh):
    in_specs = (
        P(("cell", "donor"), "gene"),
        P(("cell", "donor")),
        P(("cell", "donor")),
        P(("cell", "donor"), None),
        P("gene", None),
        P(("gene", "cell", "donor"), None),
    )
    out_specs = P(None, ("gene", "cell", "donor"), None)
    return jax.shard_map(
        per_device, mesh=mesh, in_specs=in_specs, out_specs=out_specs, check_vma=False
    )
```
